32 devices in a mesh: group: 2 (over y), frame: 8 (over z, x), row: 2 (over core).
Axes of the slice: x: 2, y: 2, z: 4, core: 2. Of those that a mesh axis runs over, the one named last changes fastest.
Arguments:
- latents: bfloat16 [16, 8, 32, 1120], P(('group', 'frame'), 'row'), parts along dimension 0, may hold values from -24 to 24
- spatial_weights: bfloat16 [4, 10, 112, 112], replicated, may hold values from -0.5 to 0.5
- causal_weights: bfloat16 [4, 10, 112, 112], replicated, may hold values from -0.5 to 0.5
Outputs:
- updated_latents: bfloat16 [16, 8, 32, 1120], P(('group', 'frame'), None, None, 'row'), parts along dimension 0
The draws below stay inside these ranges and needn't reach their ends.
There are 2 independent parts, one for each index of `group`. The reference program is written for one: setup_inputs(seed, part) draws one part's arguments, and reference() takes and returns one part's arrays. A program takes and returns all parts, laid end to end along the dimension named above; an argument that names none is the same for every part. Nothing has to cross between parts.
All inputs are finite; a program needn't handle non-finite values.
Results may differ from the reference program's by a relative error of at most 0.0047.
The reference program's roundings to bfloat16 on the way count: a program that leaves them out, or rounds other values in their place, can miss the bound.
Values may be sent and summed in bfloat16 or wider, within the bound.
A program may use at most 64 MiB of HBM per device.

```python
import jax
import jax.numpy as jnp
from jax import lax

HEADS = 10
HEAD_DIM = 112
WIDTH = 1120
COLS = 32
BAND_ROWS = 4
ROWS = 8
FRAMES = 8
N_ROW = 2


def draw_latents(key, part):
    keys = jax.random.split(jax.random.fold_in(key, 7001), 4)
    band_count = ROWS // BAND_ROWS
    ranks = 3
    frame_ids = jnp.arange(FRAMES, dtype=jnp.int32)
    fresh = jax.random.randint(keys[0], (FRAMES,), 0, 10) < 3
    fresh = jnp.logical_or(fresh, frame_ids == 0).astype(jnp.int32)
    segment = (jnp.cumsum(fresh) - 1).astype(jnp.int32)
    directions = jnp.clip(jax.random.normal(keys[1], (FRAMES, band_count, ranks, WIDTH), jnp.float32), -3.0, 3.0)
    picked = jnp.take(directions, segment, axis=0)
    weights_tok = jnp.clip(jax.random.normal(keys[2], (FRAMES, band_count, BAND_ROWS, COLS, ranks), jnp.float32), -3.0, 3.0)
    noise = jnp.clip(jax.random.normal(keys[3], (FRAMES, ROWS, COLS, WIDTH), jnp.float32), -4.0, 4.0)
    amplitude = 0.6
    structure = jnp.einsum('fbrcj,fbjw->fbrcw', weights_tok, picked).reshape(FRAMES, ROWS, COLS, WIDTH)
    return jnp.clip(noise + amplitude * structure, -24.0, 24.0).astype(jnp.bfloat16)


def centred(key, shape, width, reach, kind=jnp.bfloat16):
    entries = width * jax.random.normal(key, shape, jnp.float32)
    return jnp.clip(entries, min=-reach, max=reach).astype(kind)


def setup_inputs(seed: int = 0, part: int = 0) -> dict:
    key_of = jax.random.split(jax.random.key(seed), 4)
    part_splits = jax.random.split(jax.random.fold_in(key_of[3], part), 4)
    return {
        "latents": draw_latents(jax.random.fold_in(jax.random.fold_in(key_of[3], part), 71), part),
        "spatial_weights": centred(key_of[1], (4, HEADS, HEAD_DIM, HEAD_DIM), HEAD_DIM ** -0.5, 0.5),
        "causal_weights": centred(key_of[2], (4, HEADS, HEAD_DIM, HEAD_DIM), HEAD_DIM ** -0.5, 0.5),
    }


def project(frame_block, weights):
    flat_rows = frame_block.reshape(-1, HEADS * HEAD_DIM).astype(jnp.float32)
    normed = (flat_rows * lax.rsqrt(lax.optimization_barrier(jnp.mean(flat_rows * flat_rows, axis=-1, keepdims=True)) + 1e-06)).astype(jnp.bfloat16)
    normed = normed.reshape(-1, HEADS, HEAD_DIM).astype(jnp.float32)
    mapped = jnp.einsum('thd,khde->kthe', normed, weights.astype(jnp.float32))
    queries = jax.nn.relu(mapped[0]).astype(jnp.bfloat16)
    key_rows = jax.nn.relu(mapped[1]).astype(jnp.bfloat16)
    value_rows = mapped[2].astype(jnp.bfloat16)
    gating = jax.nn.sigmoid(mapped[3])
    return (queries, key_rows, value_rows, gating)

def band_states(frame_block, weights):
    _, key_rows, value_rows, _ = project(frame_block, weights)
    key_bands = key_rows.reshape(N_ROW, BAND_ROWS * COLS, HEADS, HEAD_DIM).astype(jnp.float32)
    value_bands = value_rows.reshape(N_ROW, BAND_ROWS * COLS, HEADS, HEAD_DIM).astype(jnp.float32)
    return jnp.einsum('bthd,bthe->bhde', key_bands, value_bands)

def finish_frame(frame_block, weights, states):
    queries, _, _, gating = project(frame_block, weights)
    query_bands = queries.reshape(N_ROW, BAND_ROWS * COLS, HEADS, HEAD_DIM).astype(jnp.float32)
    attended = jnp.einsum('bthd,bhde->bthe', query_bands, states, precision=lax.Precision.HIGHEST)
    attended = attended.reshape(-1, HEADS, HEAD_DIM)
    inv_rms = lax.rsqrt(lax.optimization_barrier(jnp.mean(attended * attended, axis=-1, keepdims=True)) + 1e-05)
    branch = (gating * attended * inv_rms).reshape(frame_block.shape)
    return (frame_block.astype(jnp.float32) + branch).astype(jnp.bfloat16)

def reference(latents, spatial_weights, causal_weights):
    spatial_bands = lax.map(lambda frame_block: band_states(frame_block, spatial_weights), latents)
    whole_frame = jnp.broadcast_to(lax.optimization_barrier(jnp.sum(spatial_bands, axis=1, keepdims=True)), spatial_bands.shape)
    mixed_video = lax.map(lambda pair: finish_frame(pair[0], spatial_weights, pair[1]), (latents, whole_frame))
    causal_bands = lax.map(lambda frame_block: band_states(frame_block, causal_weights), mixed_video)
    causal_whole = lax.optimization_barrier(jnp.sum(causal_bands, axis=1, keepdims=True))
    prefix = jnp.broadcast_to(jnp.cumsum(causal_whole, axis=0), causal_bands.shape)
    return lax.map(lambda pair: finish_frame(pair[0], causal_weights, pair[1]), (mixed_video, prefix))
```

```python
import functools

import jax
import jax.numpy as jnp
from jax import lax
from jax.experimental import pallas as pl
from jax.experimental.pallas import tpu as pltpu
from jax.sharding import PartitionSpec as P

MESH = pl.DeviceIdType.MESH
LANES = 128


def columns_of(mesh):
    count = mesh.shape["frame"]
    line = mesh.devices.reshape(mesh.shape["group"], count, mesh.shape["row"])[0, :, 0]
    places = [getattr(d, "coords", None) for d in line]
    if any(p is None or len(p) < 3 for p in places):
        return 2 if count % 2 == 0 else 1
    cols = 1
    while cols < count and places[cols][2] == places[0][2]:
        cols += 1
    return cols if count % cols == 0 else 1


def dot(a, b):
    return jnp.dot(a, b, preferred_element_type=jnp.float32)


def dot_t(a, b):
    return lax.dot_general(a, b, (((0,), (0,)), ((), ())), preferred_element_type=jnp.float32)


def kernel(nrow, ncol, nz, lat, sw, cw, out, xall, wsv, wcv, xh, nh, sq, sx, zin, zout, qs, gs, own, ob,
           lsem, xsend, xrecv, qsend, qrecv, ssend, srecv, zsend, zrecv):
    heads, toks, _ = xh.shape
    size = wsv.shape[2]
    width = heads * nrow * size
    part = toks // nrow
    r = lax.axis_index("row")
    f = lax.axis_index("frame")
    z, x = lax.div(f, ncol), lax.rem(f, ncol)

    rows_peers = [lax.rem(r + d, nrow) for d in range(1, nrow)]
    col_peers = [z * ncol + lax.rem(x + d, ncol) for d in range(1, ncol)]

    barrier = pltpu.get_barrier_semaphore()
    for p in rows_peers:
        pl.semaphore_signal(barrier, inc=1, device_id={"row": p}, device_id_type=MESH)
    for p in col_peers:
        pl.semaphore_signal(barrier, inc=1, device_id={"frame": p}, device_id_type=MESH)

    @pl.when(z > 0)
    def _():
        pl.semaphore_signal(barrier, inc=1, device_id={"frame": f - ncol}, device_id_type=MESH)

    @pl.when(z < nz - 1)
    def _():
        pl.semaphore_signal(barrier, inc=1, device_id={"frame": f + ncol}, device_id_type=MESH)

    get_x = pltpu.make_async_copy(lat.at[0], xall.at[r], lsem.at[0])
    get_s = pltpu.make_async_copy(sw.at[:, pl.ds(r * heads, heads)], wsv, lsem.at[1])
    get_c = pltpu.make_async_copy(cw.at[:, pl.ds(r * heads, heads)], wcv, lsem.at[2])
    get_x.start()
    get_s.start()
    get_c.start()

    @pl.when(z == 0)
    def _():
        zin[...] = jnp.zeros_like(zin)

    ends = jnp.where(z > 0, 1, 0) + jnp.where(z < nz - 1, 1, 0)
    pl.semaphore_wait(barrier, (nrow - 1) + (ncol - 1) + ends)

    swap_x = []
    for i, p in enumerate(rows_peers):
        c = pltpu.make_async_remote_copy(
            src_ref=lat.at[0], dst_ref=xall.at[r], send_sem=xsend.at[i], recv_sem=xrecv.at[i],
            device_id={"row": p}, device_id_type=MESH)
        c.start()
        swap_x.append(c)

    pad = jnp.zeros((part, LANES - size), jnp.bfloat16)

    def take(slot):
        start = pl.multiple_of(slot * part, part)
        v = xall[slot].reshape(part, width)
        vf = v.astype(jnp.float32)
        inv = lax.rsqrt(jnp.sum(vf * vf, axis=-1, keepdims=True) * (1.0 / width) + 1e-06)
        for rr in range(nrow):
            @pl.when(r == rr)
            def _():
                for j in range(heads):
                    lo = (rr * heads + j) * size
                    piece = v[:, lo:lo + size]
                    normed = (piece.astype(jnp.float32) * inv).astype(jnp.bfloat16)
                    xh[j, pl.ds(start, part), :] = jnp.concatenate([piece, pad], axis=1)
                    nh[j, pl.ds(start, part), :] = jnp.concatenate([normed, pad], axis=1)

    get_x.wait()
    take(r)
    get_s.wait()
    for i, c in enumerate(swap_x):
        c.wait_recv()
        take(lax.rem(r + (nrow - 1 - i), nrow))

    wpad = jnp.zeros((size, LANES - size), jnp.bfloat16)

    def project(u, w, j):
        joined = jnp.concatenate([t for k in range(4) for t in (w[k, j], wpad)], axis=1)
        m = dot(u[:, :size], joined)
        q = jnp.maximum(m[:, :LANES], 0.0).astype(jnp.bfloat16)
        k = jnp.maximum(m[:, LANES:2 * LANES], 0.0).astype(jnp.bfloat16)
        v = m[:, 2 * LANES:3 * LANES].astype(jnp.bfloat16)
        g = jax.nn.sigmoid(m[:, 3 * LANES:])
        return q, k, v, g

    def attend(q, state):
        hi = state.astype(jnp.bfloat16)
        low = (state - hi.astype(jnp.float32)).astype(jnp.bfloat16)
        return dot(jnp.concatenate([q, q], axis=1), jnp.concatenate([hi, low], axis=0))

    def finish(base, g, a):
        inv = lax.rsqrt(jnp.sum(a * a, axis=-1, keepdims=True) * (1.0 / size) + 1e-05)
        return (base.astype(jnp.float32) + g * a * inv).astype(jnp.bfloat16)

    total = jnp.zeros((toks, LANES), jnp.float32)
    for j in range(heads):
        q, k, v, g = project(nh[j], wsv, j)
        mixed = finish(xh[j], g, attend(q, dot_t(k, v)))
        xh[j] = mixed
        mf = mixed.astype(jnp.float32)
        total = total + mf * mf
    sq[r] = jnp.broadcast_to(jnp.sum(total, axis=-1, keepdims=True), (toks, LANES))

    swap_q = []
    for i, p in enumerate(rows_peers):
        c = pltpu.make_async_remote_copy(
            src_ref=sq.at[r], dst_ref=sq.at[r], send_sem=qsend.at[i], recv_sem=qrecv.at[i],
            device_id={"row": p}, device_id_type=MESH)
        c.start()
        swap_q.append(c)
    get_c.wait()
    for c in swap_q:
        c.wait_recv()
    inv_c = lax.rsqrt(jnp.sum(sq[...], axis=0) * (1.0 / width) + 1e-06)

    swap_s = []
    for j in range(heads):
        u = (xh[j].astype(jnp.float32) * inv_c).astype(jnp.bfloat16)
        q, k, v, g = project(u, wcv, j)
        state = dot_t(k, v)
        sx[x, j] = state[:size].astype(jnp.bfloat16)
        for i, p in enumerate(col_peers):
            c = pltpu.make_async_remote_copy(
                src_ref=sx.at[x, j], dst_ref=sx.at[x, j], send_sem=ssend.at[i, j], recv_sem=srecv.at[i, j],
                device_id={"frame": p}, device_id_type=MESH)
            c.start()
            swap_s.append((j, c))
        own[j] = state
        qs[j] = q
        gs[j] = g

    def chain(j):
        return pltpu.make_async_remote_copy(
            src_ref=zout.at[j], dst_ref=zin.at[j], send_sem=zsend.at[j], recv_sem=zrecv.at[j],
            device_id={"frame": lax.rem(f + ncol, ncol * nz)}, device_id_type=MESH)

    for j in range(heads):
        for jj, c in swap_s:
            if jj == j:
                c.wait_recv()

        @pl.when(z > 0)
        def _():
            chain(j).wait_recv()

        earlier = zin[j].astype(jnp.float32)
        here = earlier
        for c in range(ncol):
            t = sx[c, j].astype(jnp.float32)
            here = here + t
            earlier = earlier + jnp.where(c < x, t, 0.0)

        @pl.when(z < nz - 1)
        def _():
            zout[j] = here.astype(jnp.bfloat16)
            chain(j).start()

        full = own[j] + jnp.concatenate([earlier, jnp.zeros((LANES - size, LANES), jnp.float32)], axis=0)
        ob[j] = finish(xh[j], gs[j], attend(qs[j], full))

    done = jnp.concatenate([ob[j][:, :size] for j in range(heads)], axis=1)
    out[0] = done.reshape(out.shape[1:])

    for c in swap_x + swap_q + [c for _, c in swap_s]:
        c.wait_send()

    @pl.when(z < nz - 1)
    def _():
        for j in range(heads):
            chain(j).wait_send()


def solution(mesh):
    nrow, count = mesh.shape["row"], mesh.shape["frame"]
    ncol = columns_of(mesh)
    nz = count // ncol

    def body(latents, spatial_weights, causal_weights):
        _, band, cols, width = latents.shape
        maps, all_heads, size, _ = spatial_weights.shape
        heads = all_heads // nrow
        toks = nrow * band * cols
        bf, f32 = jnp.bfloat16, jnp.float32
        dma = pltpu.SemaphoreType.DMA
        peers, links = max(nrow - 1, 1), max(ncol - 1, 1)
        return pl.pallas_call(
            functools.partial(kernel, nrow, ncol, nz),
            out_shape=jax.ShapeDtypeStruct((1, band * nrow, cols, width // nrow), bf),
            in_specs=[pl.BlockSpec(memory_space=pl.ANY)] * 3,
            out_specs=pl.BlockSpec(memory_space=pltpu.VMEM),
            scratch_shapes=[
                pltpu.VMEM((nrow, band, cols, width), bf),
                pltpu.VMEM((maps, heads, size, size), bf),
                pltpu.VMEM((maps, heads, size, size), bf),
                pltpu.VMEM((heads, toks, LANES), bf),
                pltpu.VMEM((heads, toks, LANES), bf),
                pltpu.VMEM((nrow, toks, LANES), f32),
                pltpu.VMEM((ncol, heads, size, LANES), bf),
                pltpu.VMEM((heads, size, LANES), bf),
                pltpu.VMEM((heads, size, LANES), bf),
                pltpu.VMEM((heads, toks, LANES), bf),
                pltpu.VMEM((heads, toks, LANES), f32),
                pltpu.VMEM((heads, LANES, LANES), f32),
                pltpu.VMEM((heads, toks, LANES), bf),
                dma((3,)),
                dma((peers,)), dma((peers,)),
                dma((peers,)), dma((peers,)),
                dma((links, heads)), dma((links, heads)),
                dma((heads,)), dma((heads,)),
            ],
            compiler_params=pltpu.CompilerParams(
                collective_id=0, has_side_effects=True, vmem_limit_bytes=32 * 1024 * 1024),
        )(latents, spatial_weights, causal_weights)

    in_specs = (P(("group", "frame"), "row", None, None), P(), P())
    out_specs = P(("group", "frame"), None, None, "row")
    return jax.shard_map(body, mesh=mesh, in_specs=in_specs, out_specs=out_specs, check_vma=False)
```

```python
import functools

import jax
import jax.numpy as jnp
from jax import lax
from jax.experimental import pallas as pl
from jax.experimental.pallas import tpu as pltpu
from jax.sharding import PartitionSpec as P

MESH = pl.DeviceIdType.MESH
LANES = 128


def columns_of(mesh):
    count = mesh.shape["frame"]
    line = mesh.devices.reshape(mesh.shape["group"], count, mesh.shape["row"])[0, :, 0]
    places = [getattr(d, "coords", None) for d in line]
    if any(p is None or len(p) < 3 for p in places):
        return 2 if count % 2 == 0 else 1
    cols = 1
    while cols < count and places[cols][2] == places[0][2]:
        cols += 1
    return cols if count % cols == 0 else 1


def dot(a, b):
    return jnp.dot(a, b, preferred_element_type=jnp.float32)


def dot_t(a, b):
    return lax.dot_general(a, b, (((0,), (0,)), ((), ())), preferred_element_type=jnp.float32)


def kernel(nrow, ncol, nz, lat, sw, cw, out, xall, wsv, wcv, wj, xh, iv, sq, sx, zin, zout, qs, ks, vs, vraw, gs, own, ob,
           lsem, xsend, xrecv, qsend, qrecv, ssend, srecv, zsend, zrecv):
    heads, toks, _ = xh.shape
    size = wsv.shape[2]
    width = heads * nrow * size
    part = toks // nrow
    r = lax.axis_index("row")
    f = lax.axis_index("frame")
    z, x = lax.div(f, ncol), lax.rem(f, ncol)

    rows_peers = [lax.rem(r + d, nrow) for d in range(1, nrow)]
    col_peers = [z * ncol + lax.rem(x + d, ncol) for d in range(1, ncol)]

    barrier = pltpu.get_barrier_semaphore()
    for p in rows_peers:
        pl.semaphore_signal(barrier, inc=1, device_id={"row": p}, device_id_type=MESH)
    for p in col_peers:
        pl.semaphore_signal(barrier, inc=1, device_id={"frame": p}, device_id_type=MESH)

    @pl.when(z > 0)
    def _():
        pl.semaphore_signal(barrier, inc=1, device_id={"frame": f - ncol}, device_id_type=MESH)

    @pl.when(z < nz - 1)
    def _():
        pl.semaphore_signal(barrier, inc=1, device_id={"frame": f + ncol}, device_id_type=MESH)

    get_x = pltpu.make_async_copy(lat.at[0], xall.at[r], lsem.at[0])
    get_s = pltpu.make_async_copy(sw.at[:, pl.ds(r * heads, heads)], wsv, lsem.at[1])
    get_c = pltpu.make_async_copy(cw.at[:, pl.ds(r * heads, heads)], wcv, lsem.at[2])
    get_x.start()
    get_s.start()
    get_c.start()

    @pl.when(z == 0)
    def _():
        zin[...] = jnp.zeros_like(zin)

    ends = jnp.where(z > 0, 1, 0) + jnp.where(z < nz - 1, 1, 0)
    pl.semaphore_wait(barrier, (nrow - 1) + (ncol - 1) + ends)

    swap_x = []
    for i, p in enumerate(rows_peers):
        c = pltpu.make_async_remote_copy(
            src_ref=lat.at[0], dst_ref=xall.at[r], send_sem=xsend.at[i], recv_sem=xrecv.at[i],
            device_id={"row": p}, device_id_type=MESH)
        c.start()
        swap_x.append(c)

    pad = jnp.zeros((part, LANES - size), jnp.bfloat16)
    wpad = jnp.zeros((size, LANES - size), jnp.bfloat16)

    def join(w, j):
        return jnp.concatenate([t for k in range(4) for t in (w[k, j], wpad)], axis=1)

    def project(u, w):
        m = dot(u[:, :size], w)
        q = jnp.maximum(m[:, :LANES], 0.0).astype(jnp.bfloat16)
        k = jnp.maximum(m[:, LANES:2 * LANES], 0.0).astype(jnp.bfloat16)
        return q, k, m[:, 2 * LANES:3 * LANES], m[:, 3 * LANES:]

    def stage(slot):
        rows = pl.ds(pl.multiple_of(slot * part, part), part)
        v = xall[slot].reshape(part, width)
        vf = v.astype(jnp.float32)
        inv = lax.rsqrt(jnp.sum(vf * vf, axis=-1, keepdims=True) * (1.0 / width) + 1e-06)
        inv = jnp.broadcast_to(inv, (part, LANES))
        iv[rows, :] = inv
        for rr in range(nrow):
            @pl.when(r == rr)
            def _():
                for j in range(heads):
                    lo = (rr * heads + j) * size
                    xh[j, rows, :] = jnp.concatenate([v[:, lo:lo + size], pad], axis=1)
        for j in range(heads):
            q, k, vv, g = project(xh[j, rows, :], wj[j])
            qs[j, rows, :] = q
            ks[j, rows, :] = k
            vs[j, rows, :] = (vv * (inv * inv)).astype(jnp.bfloat16)
            gs[j, rows, :] = jax.nn.sigmoid(g * inv)

    get_s.wait()
    for j in range(heads):
        wj[j] = join(wsv, j)
    get_x.wait()
    stage(r)
    for i, c in enumerate(swap_x):
        c.wait_recv()
        stage(lax.rem(r + (nrow - 1 - i), nrow))

    def attend(q, state):
        hi = state.astype(jnp.bfloat16)
        low = (state - hi.astype(jnp.float32)).astype(jnp.bfloat16)
        return dot(jnp.concatenate([q, q], axis=1), jnp.concatenate([hi, low], axis=0))

    def finish(base, g, a, inv):
        mean = jnp.sum(a * a, axis=-1, keepdims=True) * (1.0 / size)
        scale = inv * lax.rsqrt(mean * (inv * inv) + 1e-05)
        return (base.astype(jnp.float32) + g * a * scale).astype(jnp.bfloat16)

    total = jnp.zeros((toks, LANES), jnp.float32)
    for j in range(heads):
        mixed = finish(xh[j], gs[j], attend(qs[j], dot_t(ks[j], vs[j])), iv[...])
        xh[j] = mixed
        mf = mixed.astype(jnp.float32)
        total = total + mf * mf
    sq[r] = jnp.broadcast_to(jnp.sum(total, axis=-1, keepdims=True), (toks, LANES))

    swap_q = []
    for i, p in enumerate(rows_peers):
        c = pltpu.make_async_remote_copy(
            src_ref=sq.at[r], dst_ref=sq.at[r], send_sem=qsend.at[i], recv_sem=qrecv.at[i],
            device_id={"row": p}, device_id_type=MESH)
        c.start()
        swap_q.append(c)
    get_c.wait()
    for j in range(heads):
        q, k, vv, g = project(xh[j], join(wcv, j))
        qs[j] = q
        ks[j] = k
        vraw[j] = vv
        gs[j] = g
    for c in swap_q:
        c.wait_recv()
    inv_c = lax.rsqrt(jnp.sum(sq[...], axis=0) * (1.0 / width) + 1e-06)
    iv[...] = inv_c

    swap_s = []
    for j in range(heads):
        state = dot_t(ks[j], (vraw[j] * (inv_c * inv_c)).astype(jnp.bfloat16))
        sx[x, j] = state[:size].astype(jnp.bfloat16)
        for i, p in enumerate(col_peers):
            c = pltpu.make_async_remote_copy(
                src_ref=sx.at[x, j], dst_ref=sx.at[x, j], send_sem=ssend.at[i, j], recv_sem=srecv.at[i, j],
                device_id={"frame": p}, device_id_type=MESH)
            c.start()
            swap_s.append((j, c))
        own[j] = state
    for j in range(heads):
        gs[j] = jax.nn.sigmoid(gs[j] * inv_c)

    def chain(j):
        return pltpu.make_async_remote_copy(
            src_ref=zout.at[j], dst_ref=zin.at[j], send_sem=zsend.at[j], recv_sem=zrecv.at[j],
            device_id={"frame": lax.rem(f + ncol, ncol * nz)}, device_id_type=MESH)

    for j in range(heads):
        for jj, c in swap_s:
            if jj == j:
                c.wait_recv()

        @pl.when(z > 0)
        def _():
            chain(j).wait_recv()

        earlier = zin[j].astype(jnp.float32)
        here = earlier
        for c in range(ncol):
            t = sx[c, j].astype(jnp.float32)
            here = here + t
            earlier = earlier + jnp.where(c < x, t, 0.0)

        @pl.when(z < nz - 1)
        def _():
            zout[j] = here.astype(jnp.bfloat16)
            chain(j).start()

        full = own[j] + jnp.concatenate([earlier, jnp.zeros((LANES - size, LANES), jnp.float32)], axis=0)
        ob[j] = finish(xh[j], gs[j], attend(qs[j], full), iv[...])

    done = jnp.concatenate([ob[j][:, :size] for j in range(heads)], axis=1)
    out[0] = done.reshape(out.shape[1:])

    for c in swap_x + swap_q + [c for _, c in swap_s]:
        c.wait_send()

    @pl.when(z < nz - 1)
    def _():
        for j in range(heads):
            chain(j).wait_send()


def solution(mesh):
    nrow, count = mesh.shape["row"], mesh.shape["frame"]
    ncol = columns_of(mesh)
    nz = count // ncol

    def body(latents, spatial_weights, causal_weights):
        _, band, cols, width = latents.shape
        maps, all_heads, size, _ = spatial_weights.shape
        heads = all_heads // nrow
        toks = nrow * band * cols
        bf, f32 = jnp.bfloat16, jnp.float32
        dma = pltpu.SemaphoreType.DMA
        peers, links = max(nrow - 1, 1), max(ncol - 1, 1)
        return pl.pallas_call(
            functools.partial(kernel, nrow, ncol, nz),
            out_shape=jax.ShapeDtypeStruct((1, band * nrow, cols, width // nrow), bf),
            in_specs=[pl.BlockSpec(memory_space=pltpu.HBM)] * 3,
            out_specs=pl.BlockSpec(memory_space=pltpu.VMEM),
            scratch_shapes=[
                pltpu.VMEM((nrow, band, cols, width), bf),
                pltpu.VMEM((maps, heads, size, size), bf),
                pltpu.VMEM((maps, heads, size, size), bf),
                pltpu.VMEM((heads, size, maps * LANES), bf),
                pltpu.VMEM((heads, toks, LANES), bf),
                pltpu.VMEM((toks, LANES), f32),
                pltpu.VMEM((nrow, toks, LANES), f32),
                pltpu.VMEM((ncol, heads, size, LANES), bf),
                pltpu.VMEM((heads, size, LANES), bf),
                pltpu.VMEM((heads, size, LANES), bf),
                pltpu.VMEM((heads, toks, LANES), bf),
                pltpu.VMEM((heads, toks, LANES), bf),
                pltpu.VMEM((heads, toks, LANES), bf),
                pltpu.VMEM((heads, toks, LANES), f32),
                pltpu.VMEM((heads, toks, LANES), f32),
                pltpu.VMEM((heads, LANES, LANES), f32),
                pltpu.VMEM((heads, toks, LANES), bf),
                dma((3,)),
                dma((peers,)), dma((peers,)),
                dma((peers,)), dma((peers,)),
                dma((links, heads)), dma((links, heads)),
                dma((heads,)), dma((heads,)),
            ],
            compiler_params=pltpu.CompilerParams(
                collective_id=0, has_side_effects=True, vmem_limit_bytes=32 * 1024 * 1024),
        )(latents, spatial_weights, causal_weights)

    in_specs = (P(("group", "frame"), "row", None, None), P(), P())
    out_specs = P(("group", "frame"), None, None, "row")
    return jax.shard_map(body, mesh=mesh, in_specs=in_specs, out_specs=out_specs, check_vma=False)
```

```python
import functools

import jax
import jax.numpy as jnp
from jax import lax
from jax.experimental import pallas as pl
from jax.experimental.pallas import tpu as pltpu
from jax.sharding import PartitionSpec as P

MESH = pl.DeviceIdType.MESH
LANES = 128


def columns_of(mesh):
    count = mesh.shape["frame"]
    line = mesh.devices.reshape(mesh.shape["group"], count, mesh.shape["row"])[0, :, 0]
    places = [getattr(d, "coords", None) for d in line]
    if any(p is None or len(p) < 3 for p in places):
        return 2 if count % 2 == 0 else 1
    cols = 1
    while cols < count and places[cols][2] == places[0][2]:
        cols += 1
    return cols if count % cols == 0 else 1


def dot(a, b):
    return jnp.dot(a, b, preferred_element_type=jnp.float32)


def dot_t(a, b):
    return lax.dot_general(a, b, (((0,), (0,)), ((), ())), preferred_element_type=jnp.float32)


def kernel(nrow, ncol, nz, lat, sw, cw, out, xall, wsv, wcv, wj, xh, iv, sq, sx, zin, zout, qs, ks, vs, vraw, gs, own,
           lsem, xsend, xrecv, qsend, qrecv, ssend, srecv, zsend, zrecv):
    heads, toks, _ = xh.shape
    size = wsv.shape[2]
    width = heads * nrow * size
    part = toks // nrow
    r = lax.axis_index("row")
    f = lax.axis_index("frame")
    z, x = lax.div(f, ncol), lax.rem(f, ncol)

    rows_peers = [lax.rem(r + d, nrow) for d in range(1, nrow)]
    col_peers = [z * ncol + lax.rem(x + d, ncol) for d in range(1, ncol)]

    barrier = pltpu.get_barrier_semaphore()
    for p in rows_peers:
        pl.semaphore_signal(barrier, inc=1, device_id={"row": p}, device_id_type=MESH)
    for p in col_peers:
        pl.semaphore_signal(barrier, inc=1, device_id={"frame": p}, device_id_type=MESH)

    @pl.when(z > 0)
    def _():
        pl.semaphore_signal(barrier, inc=1, device_id={"frame": f - ncol}, device_id_type=MESH)

    @pl.when(z < nz - 1)
    def _():
        pl.semaphore_signal(barrier, inc=1, device_id={"frame": f + ncol}, device_id_type=MESH)

    get_x = pltpu.make_async_copy(lat.at[0], xall.at[r], lsem.at[0])
    get_s = pltpu.make_async_copy(sw.at[:, pl.ds(r * heads, heads)], wsv, lsem.at[1])
    get_c = pltpu.make_async_copy(cw.at[:, pl.ds(r * heads, heads)], wcv, lsem.at[2])
    get_x.start()
    get_s.start()
    get_c.start()

    @pl.when(z == 0)
    def _():
        zin[...] = jnp.zeros_like(zin)

    ends = jnp.where(z > 0, 1, 0) + jnp.where(z < nz - 1, 1, 0)
    pl.semaphore_wait(barrier, (nrow - 1) + (ncol - 1) + ends)

    swap_x = []
    for i, p in enumerate(rows_peers):
        c = pltpu.make_async_remote_copy(
            src_ref=lat.at[0], dst_ref=xall.at[r], send_sem=xsend.at[i], recv_sem=xrecv.at[i],
            device_id={"row": p}, device_id_type=MESH)
        c.start()
        swap_x.append(c)

    pad = jnp.zeros((part, LANES - size), jnp.bfloat16)
    wpad = jnp.zeros((size, LANES - size), jnp.bfloat16)

    def join(w, j):
        return jnp.concatenate([t for k in range(4) for t in (w[k, j], wpad)], axis=1)

    def project(u, w):
        m = dot(u[:, :size], w)
        q = jnp.maximum(m[:, :LANES], 0.0).astype(jnp.bfloat16)
        k = jnp.maximum(m[:, LANES:2 * LANES], 0.0).astype(jnp.bfloat16)
        return q, k, m[:, 2 * LANES:3 * LANES], m[:, 3 * LANES:]

    def stage(slot):
        rows = pl.ds(pl.multiple_of(slot * part, part), part)
        v = xall[slot].reshape(part, width)
        vf = v.astype(jnp.float32)
        inv = lax.rsqrt(jnp.sum(vf * vf, axis=-1, keepdims=True) * (1.0 / width) + 1e-06)
        inv = jnp.broadcast_to(inv, (part, LANES))
        iv[rows, :] = inv
        for rr in range(nrow):
            @pl.when(r == rr)
            def _():
                for j in range(heads):
                    lo = (rr * heads + j) * size
                    xh[j, rows, :] = jnp.concatenate([v[:, lo:lo + size], pad], axis=1)
        for j in range(heads):
            q, k, vv, g = project(xh[j, rows, :], wj[j])
            qs[j, rows, :] = q
            ks[j, rows, :] = k
            vs[j, rows, :] = (vv * (inv * inv)).astype(jnp.bfloat16)
            gs[j, rows, :] = jax.nn.sigmoid(g * inv)

    get_s.wait()
    for j in range(heads):
        wj[j] = join(wsv, j)
    get_x.wait()
    stage(r)
    for i, c in enumerate(swap_x):
        c.wait_recv()
        stage(lax.rem(r + (nrow - 1 - i), nrow))

    def attend(q, state):
        hi = state.astype(jnp.bfloat16)
        low = (state - hi.astype(jnp.float32)).astype(jnp.bfloat16)
        return dot(jnp.concatenate([q, q], axis=1), jnp.concatenate([hi, low], axis=0))

    def finish(base, g, a, inv):
        mean = jnp.sum(a * a, axis=-1, keepdims=True) * (1.0 / size)
        scale = inv * lax.rsqrt(mean * (inv * inv) + 1e-05)
        return (base.astype(jnp.float32) + g * a * scale).astype(jnp.bfloat16)

    total = jnp.zeros((toks, LANES), jnp.float32)
    for j in range(heads):
        mixed = finish(xh[j], gs[j], attend(qs[j], dot_t(ks[j], vs[j])), iv[...])
        xh[j] = mixed
        mf = mixed.astype(jnp.float32)
        total = total + mf * mf
    sq[r] = jnp.broadcast_to(jnp.sum(total, axis=-1, keepdims=True), (toks, LANES))

    swap_q = []
    for i, p in enumerate(rows_peers):
        c = pltpu.make_async_remote_copy(
            src_ref=sq.at[r], dst_ref=sq.at[r], send_sem=qsend.at[i], recv_sem=qrecv.at[i],
            device_id={"row": p}, device_id_type=MESH)
        c.start()
        swap_q.append(c)
    get_c.wait()
    for j in range(heads):
        q, k, vv, g = project(xh[j], join(wcv, j))
        qs[j] = q
        ks[j] = k
        vraw[j] = vv
        gs[j] = g
    for c in swap_q:
        c.wait_recv()
    inv_c = lax.rsqrt(jnp.sum(sq[...], axis=0) * (1.0 / width) + 1e-06)
    iv[...] = inv_c

    cut = (size // 2 + 15) // 16 * 16
    chunks = [(0, cut), (cut, size - cut)]

    def share(j, h, i):
        rows = pl.ds(*chunks[h])
        return pltpu.make_async_remote_copy(
            src_ref=sx.at[x, j, rows], dst_ref=sx.at[x, j, rows], send_sem=ssend.at[i, j, h],
            recv_sem=srecv.at[i, j, h], device_id={"frame": col_peers[i]}, device_id_type=MESH)

    def chain(j, h):
        rows = pl.ds(*chunks[h])
        return pltpu.make_async_remote_copy(
            src_ref=zout.at[j, rows], dst_ref=zin.at[j, rows], send_sem=zsend.at[j, h],
            recv_sem=zrecv.at[j, h], device_id={"frame": lax.rem(f + ncol, ncol * nz)}, device_id_type=MESH)

    for j in range(heads):
        state = dot_t(ks[j], (vraw[j] * (inv_c * inv_c)).astype(jnp.bfloat16))
        sx[x, j] = state[:size].astype(jnp.bfloat16)
        for h in range(2):
            for i in range(ncol - 1):
                share(j, h, i).start()
        own[j] = state

    def arrive(j, h):
        for i in range(ncol - 1):
            share(j, h, i).wait_recv()

        @pl.when(z > 0)
        def _():
            chain(j, h).wait_recv()

    @pl.when(z < nz - 1)
    def _():
        for j in range(heads):
            for h in range(2):
                arrive(j, h)
                rows = pl.ds(*chunks[h])
                here = zin[j, rows].astype(jnp.float32)
                for c in range(ncol):
                    here = here + sx[c, j, rows].astype(jnp.float32)
                zout[j, rows] = here.astype(jnp.bfloat16)
                chain(j, h).start()

    for j in range(heads):
        gs[j] = jax.nn.sigmoid(gs[j] * inv_c)

    for j in range(heads):
        @pl.when(z == nz - 1)
        def _():
            for h in range(2):
                arrive(j, h)

        earlier = zin[j].astype(jnp.float32)
        for c in range(ncol):
            earlier = earlier + jnp.where(c < x, sx[c, j].astype(jnp.float32), 0.0)
        full = own[j] + jnp.concatenate([earlier, jnp.zeros((LANES - size, LANES), jnp.float32)], axis=0)
        done = finish(xh[j], gs[j], attend(qs[j], full), iv[...])
        out[0, :, :, j * size:(j + 1) * size] = done[:, :size].reshape(out.shape[1:3] + (size,))

    for c in swap_x + swap_q:
        c.wait_send()
    for j in range(heads):
        for h in range(2):
            for i in range(ncol - 1):
                share(j, h, i).wait_send()

    @pl.when(z < nz - 1)
    def _():
        for j in range(heads):
            for h in range(2):
                chain(j, h).wait_send()


def solution(mesh):
    nrow, count = mesh.shape["row"], mesh.shape["frame"]
    ncol = columns_of(mesh)
    nz = count // ncol

    def body(latents, spatial_weights, causal_weights):
        _, band, cols, width = latents.shape
        maps, all_heads, size, _ = spatial_weights.shape
        heads = all_heads // nrow
        toks = nrow * band * cols
        bf, f32 = jnp.bfloat16, jnp.float32
        dma = pltpu.SemaphoreType.DMA
        peers, links = max(nrow - 1, 1), max(ncol - 1, 1)
        return pl.pallas_call(
            functools.partial(kernel, nrow, ncol, nz),
            out_shape=jax.ShapeDtypeStruct((1, band * nrow, cols, width // nrow), bf),
            in_specs=[pl.BlockSpec(memory_space=pltpu.HBM)] * 3,
            out_specs=pl.BlockSpec(memory_space=pltpu.VMEM),
            scratch_shapes=[
                pltpu.VMEM((nrow, band, cols, width), bf),
                pltpu.VMEM((maps, heads, size, size), bf),
                pltpu.VMEM((maps, heads, size, size), bf),
                pltpu.VMEM((heads, size, maps * LANES), bf),
                pltpu.VMEM((heads, toks, LANES), bf),
                pltpu.VMEM((toks, LANES), f32),
                pltpu.VMEM((nrow, toks, LANES), f32),
                pltpu.VMEM((ncol, heads, size, LANES), bf),
                pltpu.VMEM((heads, size, LANES), bf),
                pltpu.VMEM((heads, size, LANES), bf),
                pltpu.VMEM((heads, toks, LANES), bf),
                pltpu.VMEM((heads, toks, LANES), bf),
                pltpu.VMEM((heads, toks, LANES), bf),
                pltpu.VMEM((heads, toks, LANES), f32),
                pltpu.VMEM((heads, toks, LANES), f32),
                pltpu.VMEM((heads, LANES, LANES), f32),
                dma((3,)),
                dma((peers,)), dma((peers,)),
                dma((peers,)), dma((peers,)),
                dma((links, heads, 2)), dma((links, heads, 2)),
                dma((heads, 2)), dma((heads, 2)),
            ],
            compiler_params=pltpu.CompilerParams(
                collective_id=0, has_side_effects=True, vmem_limit_bytes=55_000_000),
        )(latents, spatial_weights, causal_weights)

    in_specs = (P(("group", "frame"), "row", None, None), P(), P())
    out_specs = P(("group", "frame"), None, None, "row")
    return jax.shard_map(body, mesh=mesh, in_specs=in_specs, out_specs=out_specs, check_vma=False)
```

```python
import functools

import jax
import jax.numpy as jnp
from jax import lax
from jax.experimental import pallas as pl
from jax.experimental.pallas import tpu as pltpu
from jax.sharding import PartitionSpec as P

MESH = pl.DeviceIdType.MESH
LANES = 128


def columns_of(mesh):
    count = mesh.shape["frame"]
    line = mesh.devices.reshape(mesh.shape["group"], count, mesh.shape["row"])[0, :, 0]
    places = [getattr(d, "coords", None) for d in line]
    if any(p is None or len(p) < 3 for p in places):
        return 2 if count % 2 == 0 else 1
    cols = 1
    while cols < count and places[cols][2] == places[0][2]:
        cols += 1
    return cols if count % cols == 0 else 1


def dot(a, b):
    return jnp.dot(a, b, preferred_element_type=jnp.float32)


def dot_t(a, b):
    return lax.dot_general(a, b, (((0,), (0,)), ((), ())), preferred_element_type=jnp.float32)


def kernel(nrow, ncol, nz, lat, sw, cw, out, xall, wsv, wcv, wj, xh, iv, sq, sx, zin, zout, qs, ks, vs, vraw, gs, own,
           lsem, xsend, xrecv, qsend, qrecv, ssend, srecv, zsend, zrecv):
    heads, toks, _ = xh.shape
    size = wsv.shape[2]
    width = heads * nrow * size
    part = toks // nrow
    r = lax.axis_index("row")
    f = lax.axis_index("frame")
    z, x = lax.div(f, ncol), lax.rem(f, ncol)

    rows_peers = [lax.rem(r + d, nrow) for d in range(1, nrow)]
    col_peers = [z * ncol + lax.rem(x + d, ncol) for d in range(1, ncol)]

    barrier = pltpu.get_barrier_semaphore()
    for p in rows_peers:
        pl.semaphore_signal(barrier, inc=1, device_id={"row": p}, device_id_type=MESH)
    for p in col_peers:
        pl.semaphore_signal(barrier, inc=1, device_id={"frame": p}, device_id_type=MESH)

    @pl.when(z > 0)
    def _():
        pl.semaphore_signal(barrier, inc=1, device_id={"frame": f - ncol}, device_id_type=MESH)

    @pl.when(z < nz - 1)
    def _():
        pl.semaphore_signal(barrier, inc=1, device_id={"frame": f + ncol}, device_id_type=MESH)

    get_x = pltpu.make_async_copy(lat.at[0], xall.at[r], lsem.at[0])
    get_s = pltpu.make_async_copy(sw.at[:, pl.ds(r * heads, heads)], wsv, lsem.at[1])
    get_c = pltpu.make_async_copy(cw.at[:, pl.ds(r * heads, heads)], wcv, lsem.at[2])
    get_x.start()
    get_s.start()
    get_c.start()

    @pl.when(z == 0)
    def _():
        zin[...] = jnp.zeros_like(zin)

    ends = jnp.where(z > 0, 1, 0) + jnp.where(z < nz - 1, 1, 0)
    pl.semaphore_wait(barrier, (nrow - 1) + (ncol - 1) + ends)

    swap_x = []
    for i, p in enumerate(rows_peers):
        c = pltpu.make_async_remote_copy(
            src_ref=lat.at[0], dst_ref=xall.at[r], send_sem=xsend.at[i], recv_sem=xrecv.at[i],
            device_id={"row": p}, device_id_type=MESH)
        c.start()
        swap_x.append(c)

    pad = jnp.zeros((part, LANES - size), jnp.bfloat16)
    wpad = jnp.zeros((size, LANES - size), jnp.bfloat16)

    def join(w, j):
        return jnp.concatenate([t for k in range(4) for t in (w[k, j], wpad)], axis=1)

    def project(u, w):
        m = dot(u[:, :size], w)
        q = jnp.maximum(m[:, :LANES], 0.0).astype(jnp.bfloat16)
        k = jnp.maximum(m[:, LANES:2 * LANES], 0.0).astype(jnp.bfloat16)
        return q, k, m[:, 2 * LANES:3 * LANES], m[:, 3 * LANES:]

    def stage(slot):
        rows = pl.ds(pl.multiple_of(slot * part, part), part)
        v = xall[slot].reshape(part, width)
        vf = v.astype(jnp.float32)
        inv = lax.rsqrt(jnp.sum(vf * vf, axis=-1, keepdims=True) * (1.0 / width) + 1e-06)
        inv = jnp.broadcast_to(inv, (part, LANES))
        iv[rows, :] = inv
        for rr in range(nrow):
            @pl.when(r == rr)
            def _():
                for j in range(heads):
                    lo = (rr * heads + j) * size
                    xh[j, rows, :] = jnp.concatenate([v[:, lo:lo + size], pad], axis=1)
        for j in range(heads):
            q, k, vv, g = project(xh[j, rows, :], wj[j])
            qs[j, rows, :] = q
            ks[j, rows, :] = k
            vs[j, rows, :] = (vv * (inv * inv)).astype(jnp.bfloat16)
            gs[j, rows, :] = jax.nn.sigmoid(g * inv)

    get_s.wait()
    for j in range(heads):
        wj[j] = join(wsv, j)
    get_x.wait()
    stage(r)
    for i, c in enumerate(swap_x):
        c.wait_recv()
        stage(lax.rem(r + (nrow - 1 - i), nrow))

    def attend(q, state):
        hi = state.astype(jnp.bfloat16)
        low = (state - hi.astype(jnp.float32)).astype(jnp.bfloat16)
        return dot(jnp.concatenate([q, q], axis=1), jnp.concatenate([hi, low], axis=0))

    def finish(base, g, a, inv):
        mean = jnp.sum(a * a, axis=-1, keepdims=True) * (1.0 / size)
        scale = inv * lax.rsqrt(mean * (inv * inv) + 1e-05)
        return (base.astype(jnp.float32) + g * a * scale).astype(jnp.bfloat16)

    total = jnp.zeros((toks, LANES), jnp.float32)
    for j in range(heads):
        mixed = finish(xh[j], gs[j], attend(qs[j], dot_t(ks[j], vs[j])), iv[...])
        xh[j] = mixed
        mf = mixed.astype(jnp.float32)
        total = total + mf * mf
    sq[r] = jnp.broadcast_to(jnp.sum(total, axis=-1, keepdims=True), (toks, LANES))

    swap_q = []
    for i, p in enumerate(rows_peers):
        c = pltpu.make_async_remote_copy(
            src_ref=sq.at[r], dst_ref=sq.at[r], send_sem=qsend.at[i], recv_sem=qrecv.at[i],
            device_id={"row": p}, device_id_type=MESH)
        c.start()
        swap_q.append(c)
    get_c.wait()
    for j in range(heads):
        q, k, vv, g = project(xh[j], join(wcv, j))
        qs[j] = q
        ks[j] = k
        vraw[j] = vv
        gs[j] = g
    for c in swap_q:
        c.wait_recv()
    inv_c = lax.rsqrt(jnp.sum(sq[...], axis=0) * (1.0 / width) + 1e-06)
    iv[...] = inv_c

    cut = (size // 2 + 15) // 16 * 16
    chunks = [(0, cut), (cut, size - cut)]

    def share(j, h, i):
        rows = pl.ds(*chunks[h])
        return pltpu.make_async_remote_copy(
            src_ref=sx.at[x, j, rows], dst_ref=sx.at[x, j, rows], send_sem=ssend.at[i, j, h],
            recv_sem=srecv.at[i, j, h], device_id={"frame": col_peers[i]}, device_id_type=MESH)

    def chain(j, h):
        rows = pl.ds(*chunks[h])
        return pltpu.make_async_remote_copy(
            src_ref=zout.at[j, rows], dst_ref=zin.at[j, rows], send_sem=zsend.at[j, h],
            recv_sem=zrecv.at[j, h], device_id={"frame": lax.rem(f + ncol, ncol * nz)}, device_id_type=MESH)

    for j in range(heads):
        state = dot_t(ks[j], (vraw[j] * (inv_c * inv_c)).astype(jnp.bfloat16))
        sx[x, j] = state[:size].astype(jnp.bfloat16)
        own[j] = state
        for h in range(2):
            for i in range(ncol - 1):
                if j > 0:
                    share(j - 1, h, i).wait_send()
                share(j, h, i).start()

    def arrive(j, h):
        for i in range(ncol - 1):
            share(j, h, i).wait_recv()

        @pl.when(z > 0)
        def _():
            chain(j, h).wait_recv()

    @pl.when(z < nz - 1)
    def _():
        for j in range(heads):
            for h in range(2):
                arrive(j, h)
                rows = pl.ds(*chunks[h])
                here = zin[j, rows].astype(jnp.float32)
                for c in range(ncol):
                    here = here + sx[c, j, rows].astype(jnp.float32)
                zout[j, rows] = here.astype(jnp.bfloat16)
                if j > 0:
                    chain(j - 1, h).wait_send()
                chain(j, h).start()

    for j in range(heads):
        gs[j] = jax.nn.sigmoid(gs[j] * inv_c)

    for j in range(heads):
        @pl.when(z == nz - 1)
        def _():
            for h in range(2):
                arrive(j, h)

        earlier = zin[j].astype(jnp.float32)
        for c in range(ncol):
            earlier = earlier + jnp.where(c < x, sx[c, j].astype(jnp.float32), 0.0)
        full = own[j] + jnp.concatenate([earlier, jnp.zeros((LANES - size, LANES), jnp.float32)], axis=0)
        done = finish(xh[j], gs[j], attend(qs[j], full), iv[...])
        out[0, :, :, j * size:(j + 1) * size] = done[:, :size].reshape(out.shape[1:3] + (size,))

    for c in swap_x + swap_q:
        c.wait_send()
    for h in range(2):
        for i in range(ncol - 1):
            share(heads - 1, h, i).wait_send()

    @pl.when(z < nz - 1)
    def _():
        for h in range(2):
            chain(heads - 1, h).wait_send()


def solution(mesh):
    nrow, count = mesh.shape["row"], mesh.shape["frame"]
    ncol = columns_of(mesh)
    nz = count // ncol

    def body(latents, spatial_weights, causal_weights):
        _, band, cols, width = latents.shape
        maps, all_heads, size, _ = spatial_weights.shape
        heads = all_heads // nrow
        toks = nrow * band * cols
        bf, f32 = jnp.bfloat16, jnp.float32
        dma = pltpu.SemaphoreType.DMA
        peers, links = max(nrow - 1, 1), max(ncol - 1, 1)
        return pl.pallas_call(
            functools.partial(kernel, nrow, ncol, nz),
            out_shape=jax.ShapeDtypeStruct((1, band * nrow, cols, width // nrow), bf),
            in_specs=[pl.BlockSpec(memory_space=pltpu.HBM)] * 3,
            out_specs=pl.BlockSpec(memory_space=pltpu.VMEM),
            scratch_shapes=[
                pltpu.VMEM((nrow, band, cols, width), bf),
                pltpu.VMEM((maps, heads, size, size), bf),
                pltpu.VMEM((maps, heads, size, size), bf),
                pltpu.VMEM((heads, size, maps * LANES), bf),
                pltpu.VMEM((heads, toks, LANES), bf),
                pltpu.VMEM((toks, LANES), f32),
                pltpu.VMEM((nrow, toks, LANES), f32),
                pltpu.VMEM((ncol, heads, size, LANES), bf),
                pltpu.VMEM((heads, size, LANES), bf),
                pltpu.VMEM((heads, size, LANES), bf),
                pltpu.VMEM((heads, toks, LANES), bf),
                pltpu.VMEM((heads, toks, LANES), bf),
                pltpu.VMEM((heads, toks, LANES), bf),
                pltpu.VMEM((heads, toks, LANES), f32),
                pltpu.VMEM((heads, toks, LANES), f32),
                pltpu.VMEM((heads, LANES, LANES), f32),
                dma((3,)),
                dma((peers,)), dma((peers,)),
                dma((peers,)), dma((peers,)),
                dma((links, heads, 2)), dma((links, heads, 2)),
                dma((heads, 2)), dma((heads, 2)),
            ],
            compiler_params=pltpu.CompilerParams(
                collective_id=0, has_side_effects=True, vmem_limit_bytes=55_000_000),
        )(latents, spatial_weights, causal_weights)

    in_specs = (P(("group", "frame"), "row", None, None), P(), P())
    out_specs = P(("group", "frame"), None, None, "row")
    return jax.shard_map(body, mesh=mesh, in_specs=in_specs, out_specs=out_specs, check_vma=False)
```

```python
import functools

import jax
import jax.numpy as jnp
from jax import lax
from jax.experimental import pallas as pl
from jax.experimental.pallas import tpu as pltpu
from jax.sharding import PartitionSpec as P

MESH = pl.DeviceIdType.MESH
LANES = 128


def columns_of(mesh):
    count = mesh.shape["frame"]
    line = mesh.devices.reshape(mesh.shape["group"], count, mesh.shape["row"])[0, :, 0]
    places = [getattr(d, "coords", None) for d in line]
    if any(p is None or len(p) < 3 for p in places):
        return 2 if count % 2 == 0 else 1
    cols = 1
    while cols < count and places[cols][2] == places[0][2]:
        cols += 1
    return cols if count % cols == 0 else 1


def dot(a, b):
    return jnp.dot(a, b, preferred_element_type=jnp.float32)


def dot_t(a, b):
    return lax.dot_general(a, b, (((0,), (0,)), ((), ())), preferred_element_type=jnp.float32)


def kernel(nrow, ncol, nz, lat, sw, cw, out, xall, wsv, wcv, wj, xh, iv, sq, sx, zin, zout, pin, pout, qs, ks, vs, vraw, gs, own,
           lsem, xsend, xrecv, qsend, qrecv, ssend, srecv, zsend, zrecv, psend, precv):
    heads, toks, _ = xh.shape
    size = wsv.shape[2]
    width = heads * nrow * size
    part = toks // nrow
    r = lax.axis_index("row")
    f = lax.axis_index("frame")
    z, x = lax.div(f, ncol), lax.rem(f, ncol)

    rows_peers = [lax.rem(r + d, nrow) for d in range(1, nrow)]
    other_cols = [lax.rem(x + d, ncol) for d in range(1, ncol)]

    owner_col = lax.rem(r, ncol)
    owner = x == owner_col
    up, down = jnp.logical_and(owner, z < nz - 1), jnp.logical_and(owner, z > 0)

    barrier = pltpu.get_barrier_semaphore()
    for p in rows_peers:
        pl.semaphore_signal(barrier, inc=1, device_id={"row": p}, device_id_type=MESH)

    @pl.when(owner)
    def _():
        for c in other_cols:
            pl.semaphore_signal(barrier, inc=1, device_id={"frame": z * ncol + c}, device_id_type=MESH)

    @pl.when(jnp.logical_not(owner))
    def _():
        pl.semaphore_signal(barrier, inc=1, device_id={"frame": z * ncol + owner_col}, device_id_type=MESH)

    @pl.when(down)
    def _():
        pl.semaphore_signal(barrier, inc=1, device_id={"frame": f - ncol}, device_id_type=MESH)

    @pl.when(up)
    def _():
        pl.semaphore_signal(barrier, inc=1, device_id={"frame": f + ncol}, device_id_type=MESH)

    get_x = pltpu.make_async_copy(lat.at[0], xall.at[r], lsem.at[0])
    get_s = pltpu.make_async_copy(sw.at[:, pl.ds(r * heads, heads)], wsv, lsem.at[1])
    get_c = pltpu.make_async_copy(cw.at[:, pl.ds(r * heads, heads)], wcv, lsem.at[2])
    get_x.start()
    get_s.start()
    get_c.start()

    @pl.when(z == 0)
    def _():
        zin[...] = jnp.zeros_like(zin)

    ends = jnp.where(z > 0, 1, 0) + jnp.where(z < nz - 1, 1, 0)
    pl.semaphore_wait(barrier, (nrow - 1) + jnp.where(owner, (ncol - 1) + ends, 1))

    swap_x = []
    for i, p in enumerate(rows_peers):
        c = pltpu.make_async_remote_copy(
            src_ref=lat.at[0], dst_ref=xall.at[r], send_sem=xsend.at[i], recv_sem=xrecv.at[i],
            device_id={"row": p}, device_id_type=MESH)
        c.start()
        swap_x.append(c)

    pad = jnp.zeros((part, LANES - size), jnp.bfloat16)
    wpad = jnp.zeros((size, LANES - size), jnp.bfloat16)

    def join(w, j):
        return jnp.concatenate([t for k in range(4) for t in (w[k, j], wpad)], axis=1)

    def project(u, w):
        m = dot(u[:, :size], w)
        q = jnp.maximum(m[:, :LANES], 0.0).astype(jnp.bfloat16)
        k = jnp.maximum(m[:, LANES:2 * LANES], 0.0).astype(jnp.bfloat16)
        return q, k, m[:, 2 * LANES:3 * LANES], m[:, 3 * LANES:]

    def stage(slot):
        rows = pl.ds(pl.multiple_of(slot * part, part), part)
        v = xall[slot].reshape(part, width)
        vf = v.astype(jnp.float32)
        inv = lax.rsqrt(jnp.sum(vf * vf, axis=-1, keepdims=True) * (1.0 / width) + 1e-06)
        inv = jnp.broadcast_to(inv, (part, LANES))
        iv[rows, :] = inv
        for rr in range(nrow):
            @pl.when(r == rr)
            def _():
                for j in range(heads):
                    lo = (rr * heads + j) * size
                    xh[j, rows, :] = jnp.concatenate([v[:, lo:lo + size], pad], axis=1)
        for j in range(heads):
            q, k, vv, g = project(xh[j, rows, :], wj[j])
            qs[j, rows, :] = q
            ks[j, rows, :] = k
            vs[j, rows, :] = (vv * (inv * inv)).astype(jnp.bfloat16)
            gs[j, rows, :] = jax.nn.sigmoid(g * inv)

    get_s.wait()
    for j in range(heads):
        wj[j] = join(wsv, j)
    get_x.wait()
    stage(r)
    for i, c in enumerate(swap_x):
        c.wait_recv()
        stage(lax.rem(r + (nrow - 1 - i), nrow))

    def attend(q, state):
        hi = state.astype(jnp.bfloat16)
        low = (state - hi.astype(jnp.float32)).astype(jnp.bfloat16)
        return dot(jnp.concatenate([q, q], axis=1), jnp.concatenate([hi, low], axis=0))

    def finish(base, g, a, inv):
        mean = jnp.sum(a * a, axis=-1, keepdims=True) * (1.0 / size)
        scale = inv * lax.rsqrt(mean * (inv * inv) + 1e-05)
        return (base.astype(jnp.float32) + g * a * scale).astype(jnp.bfloat16)

    total = jnp.zeros((toks, LANES), jnp.float32)
    for j in range(heads):
        mixed = finish(xh[j], gs[j], attend(qs[j], dot_t(ks[j], vs[j])), iv[...])
        xh[j] = mixed
        mf = mixed.astype(jnp.float32)
        total = total + mf * mf
    sq[r] = jnp.broadcast_to(jnp.sum(total, axis=-1, keepdims=True), (toks, LANES))

    swap_q = []
    for i, p in enumerate(rows_peers):
        c = pltpu.make_async_remote_copy(
            src_ref=sq.at[r], dst_ref=sq.at[r], send_sem=qsend.at[i], recv_sem=qrecv.at[i],
            device_id={"row": p}, device_id_type=MESH)
        c.start()
        swap_q.append(c)
    get_c.wait()
    for j in range(heads):
        q, k, vv, g = project(xh[j], join(wcv, j))
        qs[j] = q
        ks[j] = k
        vraw[j] = vv
        gs[j] = g
    for c in swap_q:
        c.wait_recv()
    inv_c = lax.rsqrt(jnp.sum(sq[...], axis=0) * (1.0 / width) + 1e-06)
    iv[...] = inv_c

    cut = (size // 2 + 15) // 16 * 16
    chunks = [(0, cut), (cut, size - cut)]

    def share(c, j, h):
        rows = pl.ds(*chunks[h])
        return pltpu.make_async_remote_copy(
            src_ref=sx.at[c, j, rows], dst_ref=sx.at[c, j, rows], send_sem=ssend.at[j, h],
            recv_sem=srecv.at[c, j, h], device_id={"frame": z * ncol + owner_col}, device_id_type=MESH)

    def chain(j, h):
        rows = pl.ds(*chunks[h])
        return pltpu.make_async_remote_copy(
            src_ref=zout.at[j, rows], dst_ref=zin.at[j, rows], send_sem=zsend.at[j, h],
            recv_sem=zrecv.at[j, h], device_id={"frame": lax.rem(f + ncol, ncol * nz)}, device_id_type=MESH)

    def give(c, j, h):
        rows = pl.ds(*chunks[h])
        return pltpu.make_async_remote_copy(
            src_ref=pout.at[c, j, rows], dst_ref=pin.at[j, rows], send_sem=psend.at[c, j, h],
            recv_sem=precv.at[j, h], device_id={"frame": z * ncol + c}, device_id_type=MESH)

    for j in range(heads):
        state = dot_t(ks[j], (vraw[j] * (inv_c * inv_c)).astype(jnp.bfloat16))
        sx[x, j] = state[:size].astype(jnp.bfloat16)

        @pl.when(jnp.logical_not(owner))
        def _():
            for h in range(2):
                share(x, j, h).start()
        own[j] = state

    @pl.when(owner)
    def _():
        for j in range(heads):
            for h in range(2):
                rows = pl.ds(*chunks[h])
                for c in other_cols:
                    share(c, j, h).wait_recv()
                here = [sx[c, j, rows].astype(jnp.float32) for c in range(ncol)]

                @pl.when(down)
                def _():
                    chain(j, h).wait_recv()

                total = zin[j, rows].astype(jnp.float32)
                before = []
                for c in range(ncol):
                    before.append(total)
                    total = total + here[c]

                @pl.when(up)
                def _():
                    zout[j, rows] = total.astype(jnp.bfloat16)
                    chain(j, h).start()

                for c in range(ncol):
                    pout[c, j, rows] = before[c].astype(jnp.bfloat16)

                    @pl.when(c != x)
                    def _():
                        give(c, j, h).start()

    for j in range(heads):
        gs[j] = jax.nn.sigmoid(gs[j] * inv_c)
        vraw[j] = attend(qs[j], own[j])

    tail = jnp.zeros((LANES - size, LANES), jnp.bfloat16)
    for j in range(heads):
        @pl.when(owner)
        def _():
            pin[j] = pout[x, j]

        @pl.when(jnp.logical_not(owner))
        def _():
            for h in range(2):
                give(x, j, h).wait_recv()

        a = vraw[j] + dot(qs[j], jnp.concatenate([pin[j], tail], axis=0))
        done = finish(xh[j], gs[j], a, iv[...])
        out[0, :, :, j * size:(j + 1) * size] = done[:, :size].reshape(out.shape[1:3] + (size,))

    for c in swap_x + swap_q:
        c.wait_send()

    @pl.when(jnp.logical_not(owner))
    def _():
        for j in range(heads):
            for h in range(2):
                share(x, j, h).wait_send()

    @pl.when(owner)
    def _():
        for j in range(heads):
            for h in range(2):
                for c in other_cols:
                    give(c, j, h).wait_send()

    @pl.when(up)
    def _():
        for j in range(heads):
            for h in range(2):
                chain(j, h).wait_send()


def solution(mesh):
    nrow, count = mesh.shape["row"], mesh.shape["frame"]
    ncol = columns_of(mesh)
    nz = count // ncol

    def body(latents, spatial_weights, causal_weights):
        _, band, cols, width = latents.shape
        maps, all_heads, size, _ = spatial_weights.shape
        heads = all_heads // nrow
        toks = nrow * band * cols
        bf, f32 = jnp.bfloat16, jnp.float32
        dma = pltpu.SemaphoreType.DMA
        peers = max(nrow - 1, 1)
        return pl.pallas_call(
            functools.partial(kernel, nrow, ncol, nz),
            out_shape=jax.ShapeDtypeStruct((1, band * nrow, cols, width // nrow), bf),
            in_specs=[pl.BlockSpec(memory_space=pltpu.HBM)] * 3,
            out_specs=pl.BlockSpec(memory_space=pltpu.VMEM),
            scratch_shapes=[
                pltpu.VMEM((nrow, band, cols, width), bf),
                pltpu.VMEM((maps, heads, size, size), bf),
                pltpu.VMEM((maps, heads, size, size), bf),
                pltpu.VMEM((heads, size, maps * LANES), bf),
                pltpu.VMEM((heads, toks, LANES), bf),
                pltpu.VMEM((toks, LANES), f32),
                pltpu.VMEM((nrow, toks, LANES), f32),
                pltpu.VMEM((ncol, heads, size, LANES), bf),
                pltpu.VMEM((heads, size, LANES), bf),
                pltpu.VMEM((heads, size, LANES), bf),
                pltpu.VMEM((heads, size, LANES), bf),
                pltpu.VMEM((ncol, heads, size, LANES), bf),
                pltpu.VMEM((heads, toks, LANES), bf),
                pltpu.VMEM((heads, toks, LANES), bf),
                pltpu.VMEM((heads, toks, LANES), bf),
                pltpu.VMEM((heads, toks, LANES), f32),
                pltpu.VMEM((heads, toks, LANES), f32),
                pltpu.VMEM((heads, LANES, LANES), f32),
                dma((3,)),
                dma((peers,)), dma((peers,)),
                dma((peers,)), dma((peers,)),
                dma((heads, 2)), dma((ncol, heads, 2)),
                dma((heads, 2)), dma((heads, 2)),
                dma((ncol, heads, 2)), dma((heads, 2)),
            ],
            compiler_params=pltpu.CompilerParams(
                collective_id=0, has_side_effects=True, vmem_limit_bytes=55_000_000),
        )(latents, spatial_weights, causal_weights)

    in_specs = (P(("group", "frame"), "row", None, None), P(), P())
    out_specs = P(("group", "frame"), None, None, "row")
    return jax.shard_map(body, mesh=mesh, in_specs=in_specs, out_specs=out_specs, check_vma=False)
```

```python
import functools

import jax
import jax.numpy as jnp
from jax import lax
from jax.experimental import pallas as pl
from jax.experimental.pallas import tpu as pltpu
from jax.sharding import PartitionSpec as P

MESH = pl.DeviceIdType.MESH
LANES = 128


def columns_of(mesh):
    count = mesh.shape["frame"]
    line = mesh.devices.reshape(mesh.shape["group"], count, mesh.shape["row"])[0, :, 0]
    places = [getattr(d, "coords", None) for d in line]
    if any(p is None or len(p) < 3 for p in places):
        return 2 if count % 2 == 0 else 1
    cols = 1
    while cols < count and places[cols][2] == places[0][2]:
        cols += 1
    return cols if count % cols == 0 else 1


def dot(a, b):
    return jnp.dot(a, b, preferred_element_type=jnp.float32)


def dot_t(a, b):
    return lax.dot_general(a, b, (((0,), (0,)), ((), ())), preferred_element_type=jnp.float32)


def kernel(nrow, ncol, nz, lat, sw, cw, out, xall, wsv, wcv, wj, xh, iv, sq, mine, sx, zin, zout, pin, pout, qs, ks, vs, vraw, gs, own,
           lsem, xsend, xrecv, qsend, qrecv, ssend, srecv, zsend, zrecv, psend, precv):
    heads, toks, _ = xh.shape
    size = wsv.shape[2]
    width = heads * nrow * size
    part = toks // nrow
    r = lax.axis_index("row")
    f = lax.axis_index("frame")
    z, x = lax.div(f, ncol), lax.rem(f, ncol)

    rows_peers = [lax.rem(r + d, nrow) for d in range(1, nrow)]

    spread = ncol >= nrow
    my_col, my_row = lax.rem(r, ncol), (nrow - 1 if spread else r)
    at_home = jnp.logical_and(x == my_col, r == my_row)
    held = x if spread else r
    owner = jnp.logical_and(r == nrow - 1, x < nrow) if spread else x == my_col
    up, down = jnp.logical_and(owner, z < nz - 1), jnp.logical_and(owner, z > 0)
    to_owner = {"frame": z * ncol + my_col, "row": my_row}

    def client(c):
        return {"frame": z * ncol + c, "row": lax.rem(held, nrow)}

    def away(c):
        return jnp.logical_not(jnp.logical_and(held == r, c == x))

    barrier = pltpu.get_barrier_semaphore()
    for p in rows_peers:
        pl.semaphore_signal(barrier, inc=1, device_id={"row": p}, device_id_type=MESH)

    @pl.when(jnp.logical_not(at_home))
    def _():
        pl.semaphore_signal(barrier, inc=1, device_id=to_owner, device_id_type=MESH)

    for c in range(ncol):
        @pl.when(jnp.logical_and(owner, away(c)))
        def _():
            pl.semaphore_signal(barrier, inc=1, device_id=client(c), device_id_type=MESH)

    @pl.when(down)
    def _():
        pl.semaphore_signal(barrier, inc=1, device_id={"frame": f - ncol}, device_id_type=MESH)

    @pl.when(up)
    def _():
        pl.semaphore_signal(barrier, inc=1, device_id={"frame": f + ncol}, device_id_type=MESH)

    get_x = pltpu.make_async_copy(lat.at[0], xall.at[r], lsem.at[0])
    get_s = pltpu.make_async_copy(sw.at[:, pl.ds(r * heads, heads)], wsv, lsem.at[1])
    get_c = pltpu.make_async_copy(cw.at[:, pl.ds(r * heads, heads)], wcv, lsem.at[2])
    get_x.start()
    get_s.start()
    get_c.start()

    @pl.when(z == 0)
    def _():
        zin[...] = jnp.zeros_like(zin)

    ends = jnp.where(z > 0, 1, 0) + jnp.where(z < nz - 1, 1, 0)
    clients = ncol - jnp.where(held == r, 1, 0)
    pl.semaphore_wait(barrier, (nrow - 1) + jnp.where(at_home, 0, 1) + jnp.where(owner, clients + ends, 0))

    swap_x = []
    for i, p in enumerate(rows_peers):
        c = pltpu.make_async_remote_copy(
            src_ref=lat.at[0], dst_ref=xall.at[r], send_sem=xsend.at[i], recv_sem=xrecv.at[i],
            device_id={"row": p}, device_id_type=MESH)
        c.start()
        swap_x.append(c)

    pad = jnp.zeros((part, LANES - size), jnp.bfloat16)
    wpad = jnp.zeros((size, LANES - size), jnp.bfloat16)

    def join(w, j):
        return jnp.concatenate([t for k in range(4) for t in (w[k, j], wpad)], axis=1)

    def project(u, w):
        m = dot(u[:, :size], w)
        q = jnp.maximum(m[:, :LANES], 0.0).astype(jnp.bfloat16)
        k = jnp.maximum(m[:, LANES:2 * LANES], 0.0).astype(jnp.bfloat16)
        return q, k, m[:, 2 * LANES:3 * LANES], m[:, 3 * LANES:]

    def stage(slot):
        rows = pl.ds(pl.multiple_of(slot * part, part), part)
        v = xall[slot].reshape(part, width)
        vf = v.astype(jnp.float32)
        inv = lax.rsqrt(jnp.sum(vf * vf, axis=-1, keepdims=True) * (1.0 / width) + 1e-06)
        inv = jnp.broadcast_to(inv, (part, LANES))
        iv[rows, :] = inv
        for rr in range(nrow):
            @pl.when(r == rr)
            def _():
                for j in range(heads):
                    lo = (rr * heads + j) * size
                    xh[j, rows, :] = jnp.concatenate([v[:, lo:lo + size], pad], axis=1)
        for j in range(heads):
            q, k, vv, g = project(xh[j, rows, :], wj[j])
            qs[j, rows, :] = q
            ks[j, rows, :] = k
            vs[j, rows, :] = (vv * (inv * inv)).astype(jnp.bfloat16)
            gs[j, rows, :] = jax.nn.sigmoid(g * inv)

    get_s.wait()
    for j in range(heads):
        wj[j] = join(wsv, j)
    get_x.wait()
    stage(r)
    for i, c in enumerate(swap_x):
        c.wait_recv()
        stage(lax.rem(r + (nrow - 1 - i), nrow))

    def attend(q, state):
        hi = state.astype(jnp.bfloat16)
        low = (state - hi.astype(jnp.float32)).astype(jnp.bfloat16)
        return dot(jnp.concatenate([q, q], axis=1), jnp.concatenate([hi, low], axis=0))

    def finish(base, g, a, inv):
        mean = jnp.sum(a * a, axis=-1, keepdims=True) * (1.0 / size)
        scale = inv * lax.rsqrt(mean * (inv * inv) + 1e-05)
        return (base.astype(jnp.float32) + g * a * scale).astype(jnp.bfloat16)

    total = jnp.zeros((toks, LANES), jnp.float32)
    for j in range(heads):
        mixed = finish(xh[j], gs[j], attend(qs[j], dot_t(ks[j], vs[j])), iv[...])
        xh[j] = mixed
        mf = mixed.astype(jnp.float32)
        total = total + mf * mf
    sq[r] = jnp.broadcast_to(jnp.sum(total, axis=-1, keepdims=True), (toks, LANES))

    swap_q = []
    for i, p in enumerate(rows_peers):
        c = pltpu.make_async_remote_copy(
            src_ref=sq.at[r], dst_ref=sq.at[r], send_sem=qsend.at[i], recv_sem=qrecv.at[i],
            device_id={"row": p}, device_id_type=MESH)
        c.start()
        swap_q.append(c)
    get_c.wait()
    for j in range(heads):
        q, k, vv, g = project(xh[j], join(wcv, j))
        qs[j] = q
        ks[j] = k
        vraw[j] = vv
        gs[j] = g
    for c in swap_q:
        c.wait_recv()
    inv_c = lax.rsqrt(jnp.sum(sq[...], axis=0) * (1.0 / width) + 1e-06)
    iv[...] = inv_c

    cut = (size // 2 + 15) // 16 * 16
    chunks = [(0, cut), (cut, size - cut)]

    def share(c, j, h):
        rows = pl.ds(*chunks[h])
        return pltpu.make_async_remote_copy(
            src_ref=mine.at[j, rows], dst_ref=sx.at[c, j, rows], send_sem=ssend.at[j, h],
            recv_sem=srecv.at[c, j, h], device_id=to_owner, device_id_type=MESH)

    def chain(j, h):
        rows = pl.ds(*chunks[h])
        return pltpu.make_async_remote_copy(
            src_ref=zout.at[j, rows], dst_ref=zin.at[j, rows], send_sem=zsend.at[j, h],
            recv_sem=zrecv.at[j, h], device_id={"frame": lax.rem(f + ncol, ncol * nz)}, device_id_type=MESH)

    def give(c, j, h):
        rows = pl.ds(*chunks[h])
        return pltpu.make_async_remote_copy(
            src_ref=pout.at[c, j, rows], dst_ref=pin.at[j, rows], send_sem=psend.at[c, j, h],
            recv_sem=precv.at[j, h], device_id=client(c), device_id_type=MESH)

    for j in range(heads):
        state = dot_t(ks[j], (vraw[j] * (inv_c * inv_c)).astype(jnp.bfloat16))
        mine[j] = state[:size].astype(jnp.bfloat16)

        @pl.when(at_home)
        def _():
            sx[x, j] = mine[j]

        @pl.when(jnp.logical_not(at_home))
        def _():
            for h in range(2):
                share(x, j, h).start()
        own[j] = state

    @pl.when(owner)
    def _():
        for j in range(heads):
            for h in range(2):
                rows = pl.ds(*chunks[h])
                for c in range(ncol):
                    @pl.when(away(c))
                    def _():
                        share(c, j, h).wait_recv()
                here = [sx[c, j, rows].astype(jnp.float32) for c in range(ncol)]

                @pl.when(down)
                def _():
                    chain(j, h).wait_recv()

                total = zin[j, rows].astype(jnp.float32)
                before = []
                for c in range(ncol):
                    before.append(total)
                    total = total + here[c]

                @pl.when(up)
                def _():
                    zout[j, rows] = total.astype(jnp.bfloat16)
                    chain(j, h).start()

                for c in range(ncol):
                    pout[c, j, rows] = before[c].astype(jnp.bfloat16)

                    @pl.when(away(c))
                    def _():
                        give(c, j, h).start()

    for j in range(heads):
        gs[j] = jax.nn.sigmoid(gs[j] * inv_c)
        vraw[j] = attend(qs[j], own[j])

    tail = jnp.zeros((LANES - size, LANES), jnp.bfloat16)
    for j in range(heads):
        @pl.when(at_home)
        def _():
            pin[j] = pout[x, j]

        @pl.when(jnp.logical_not(at_home))
        def _():
            for h in range(2):
                give(x, j, h).wait_recv()

        a = vraw[j] + dot(qs[j], jnp.concatenate([pin[j], tail], axis=0))
        done = finish(xh[j], gs[j], a, iv[...])
        out[0, :, :, j * size:(j + 1) * size] = done[:, :size].reshape(out.shape[1:3] + (size,))

    for c in swap_x + swap_q:
        c.wait_send()

    @pl.when(jnp.logical_not(at_home))
    def _():
        for j in range(heads):
            for h in range(2):
                share(x, j, h).wait_send()

    for c in range(ncol):
        @pl.when(jnp.logical_and(owner, away(c)))
        def _():
            for j in range(heads):
                for h in range(2):
                    give(c, j, h).wait_send()

    @pl.when(up)
    def _():
        for j in range(heads):
            for h in range(2):
                chain(j, h).wait_send()


def solution(mesh):
    nrow, count = mesh.shape["row"], mesh.shape["frame"]
    ncol = columns_of(mesh)
    nz = count // ncol

    def body(latents, spatial_weights, causal_weights):
        _, band, cols, width = latents.shape
        maps, all_heads, size, _ = spatial_weights.shape
        heads = all_heads // nrow
        toks = nrow * band * cols
        bf, f32 = jnp.bfloat16, jnp.float32
        dma = pltpu.SemaphoreType.DMA
        peers = max(nrow - 1, 1)
        return pl.pallas_call(
            functools.partial(kernel, nrow, ncol, nz),
            out_shape=jax.ShapeDtypeStruct((1, band * nrow, cols, width // nrow), bf),
            in_specs=[pl.BlockSpec(memory_space=pltpu.HBM)] * 3,
            out_specs=pl.BlockSpec(memory_space=pltpu.VMEM),
            scratch_shapes=[
                pltpu.VMEM((nrow, band, cols, width), bf),
                pltpu.VMEM((maps, heads, size, size), bf),
                pltpu.VMEM((maps, heads, size, size), bf),
                pltpu.VMEM((heads, size, maps * LANES), bf),
                pltpu.VMEM((heads, toks, LANES), bf),
                pltpu.VMEM((toks, LANES), f32),
                pltpu.VMEM((nrow, toks, LANES), f32),
                pltpu.VMEM((heads, size, LANES), bf),
                pltpu.VMEM((ncol, heads, size, LANES), bf),
                pltpu.VMEM((heads, size, LANES), bf),
                pltpu.VMEM((heads, size, LANES), bf),
                pltpu.VMEM((heads, size, LANES), bf),
                pltpu.VMEM((ncol, heads, size, LANES), bf),
                pltpu.VMEM((heads, toks, LANES), bf),
                pltpu.VMEM((heads, toks, LANES), bf),
                pltpu.VMEM((heads, toks, LANES), bf),
                pltpu.VMEM((heads, toks, LANES), f32),
                pltpu.VMEM((heads, toks, LANES), f32),
                pltpu.VMEM((heads, LANES, LANES), f32),
                dma((3,)),
                dma((peers,)), dma((peers,)),
                dma((peers,)), dma((peers,)),
                dma((heads, 2)), dma((ncol, heads, 2)),
                dma((heads, 2)), dma((heads, 2)),
                dma((ncol, heads, 2)), dma((heads, 2)),
            ],
            compiler_params=pltpu.CompilerParams(
                collective_id=0, has_side_effects=True, vmem_limit_bytes=55_000_000),
        )(latents, spatial_weights, causal_weights)

    in_specs = (P(("group", "frame"), "row", None, None), P(), P())
    out_specs = P(("group", "frame"), None, None, "row")
    return jax.shard_map(body, mesh=mesh, in_specs=in_specs, out_specs=out_specs, check_vma=False)
```

```python
import functools

import jax
import jax.numpy as jnp
from jax import lax
from jax.experimental import pallas as pl
from jax.experimental.pallas import tpu as pltpu
from jax.sharding import PartitionSpec as P

MESH = pl.DeviceIdType.MESH
LANES = 128


def columns_of(mesh):
    count = mesh.shape["frame"]
    line = mesh.devices.reshape(mesh.shape["group"], count, mesh.shape["row"])[0, :, 0]
    places = [getattr(d, "coords", None) for d in line]
    if any(p is None or len(p) < 3 for p in places):
        return 2 if count % 2 == 0 else 1
    cols = 1
    while cols < count and places[cols][2] == places[0][2]:
        cols += 1
    return cols if count % cols == 0 else 1


def dot(a, b):
    return jnp.dot(a, b, preferred_element_type=jnp.float32)


def dot_t(a, b):
    return lax.dot_general(a, b, (((0,), (0,)), ((), ())), preferred_element_type=jnp.float32)


def kernel(nrow, ncol, nz, lat, sw, cw, out, xall, wsv, wcv, wj, xh, iv, sq, mine, sx, zin, zout, pin, pout, qs, ks, vs, vraw, gs, own,
           lsem, xsend, xrecv, qsend, qrecv, ssend, srecv, zsend, zrecv, psend, precv):
    heads, toks, _ = xh.shape
    size = wsv.shape[2]
    width = heads * nrow * size
    part = toks // nrow
    r = lax.axis_index("row")
    f = lax.axis_index("frame")
    z, x = lax.div(f, ncol), lax.rem(f, ncol)

    rows_peers = [lax.rem(r + d, nrow) for d in range(1, nrow)]

    spread = ncol >= nrow
    my_col, my_row = lax.rem(r, ncol), (nrow - 1 if spread else r)
    at_home = jnp.logical_and(x == my_col, r == my_row)
    held = x if spread else r
    owner = jnp.logical_and(r == nrow - 1, x < nrow) if spread else x == my_col
    up, down = jnp.logical_and(owner, z < nz - 1), jnp.logical_and(owner, z > 0)
    to_owner = {"frame": z * ncol + my_col, "row": my_row}

    def client(c):
        return {"frame": z * ncol + c, "row": lax.rem(held, nrow)}

    def away(c):
        return jnp.logical_not(jnp.logical_and(held == r, c == x))

    barrier = pltpu.get_barrier_semaphore()
    for p in rows_peers:
        pl.semaphore_signal(barrier, inc=1, device_id={"row": p}, device_id_type=MESH)

    @pl.when(jnp.logical_not(at_home))
    def _():
        pl.semaphore_signal(barrier, inc=1, device_id=to_owner, device_id_type=MESH)

    for c in range(ncol):
        @pl.when(jnp.logical_and(owner, away(c)))
        def _():
            pl.semaphore_signal(barrier, inc=1, device_id=client(c), device_id_type=MESH)

    @pl.when(down)
    def _():
        pl.semaphore_signal(barrier, inc=1, device_id={"frame": f - ncol}, device_id_type=MESH)

    @pl.when(up)
    def _():
        pl.semaphore_signal(barrier, inc=1, device_id={"frame": f + ncol}, device_id_type=MESH)

    get_x = pltpu.make_async_copy(lat.at[0], xall.at[r], lsem.at[0])
    get_s = pltpu.make_async_copy(sw.at[:, pl.ds(r * heads, heads)], wsv, lsem.at[1])
    get_c = pltpu.make_async_copy(cw.at[:, pl.ds(r * heads, heads)], wcv, lsem.at[2])
    get_x.start()
    get_s.start()
    get_c.start()

    @pl.when(z == 0)
    def _():
        zin[...] = jnp.zeros_like(zin)

    pad = jnp.zeros((part, LANES - size), jnp.bfloat16)
    wpad = jnp.zeros((size, LANES - size), jnp.bfloat16)

    def join(w, j):
        return jnp.concatenate([t for k in range(4) for t in (w[k, j], wpad)], axis=1)

    def project(u, w):
        m = dot(u[:, :size], w)
        q = jnp.maximum(m[:, :LANES], 0.0).astype(jnp.bfloat16)
        k = jnp.maximum(m[:, LANES:2 * LANES], 0.0).astype(jnp.bfloat16)
        return q, k, m[:, 2 * LANES:3 * LANES], m[:, 3 * LANES:]

    def prepare(slot):
        rows = pl.ds(pl.multiple_of(slot * part, part), part)
        v = xall[slot].reshape(part, width)
        vf = v.astype(jnp.float32)
        inv = lax.rsqrt(jnp.sum(vf * vf, axis=-1, keepdims=True) * (1.0 / width) + 1e-06)
        iv[rows, :] = jnp.broadcast_to(inv, (part, LANES))
        for rr in range(nrow):
            @pl.when(r == rr)
            def _():
                for j in range(heads):
                    lo = (rr * heads + j) * size
                    xh[j, rows, :] = jnp.concatenate([v[:, lo:lo + size], pad], axis=1)

    def maps(slot):
        rows = pl.ds(pl.multiple_of(slot * part, part), part)
        inv = iv[rows, :]
        for j in range(heads):
            q, k, vv, g = project(xh[j, rows, :], wj[0, j])
            qs[j, rows, :] = q
            ks[j, rows, :] = k
            vs[j, rows, :] = (vv * (inv * inv)).astype(jnp.bfloat16)
            gs[j, rows, :] = jax.nn.sigmoid(g * inv)

    get_x.wait()
    prepare(r)
    get_s.wait()
    for j in range(heads):
        wj[0, j] = join(wsv, j)

    ends = jnp.where(z > 0, 1, 0) + jnp.where(z < nz - 1, 1, 0)
    clients = ncol - jnp.where(held == r, 1, 0)
    pl.semaphore_wait(barrier, (nrow - 1) + jnp.where(at_home, 0, 1) + jnp.where(owner, clients + ends, 0))

    swap_x = []
    for i, p in enumerate(rows_peers):
        c = pltpu.make_async_remote_copy(
            src_ref=lat.at[0], dst_ref=xall.at[r], send_sem=xsend.at[i], recv_sem=xrecv.at[i],
            device_id={"row": p}, device_id_type=MESH)
        c.start()
        swap_x.append(c)

    maps(r)
    get_c.wait()
    for j in range(heads):
        wj[1, j] = join(wcv, j)
    for i, c in enumerate(swap_x):
        c.wait_recv()
        prepare(lax.rem(r + (nrow - 1 - i), nrow))
        maps(lax.rem(r + (nrow - 1 - i), nrow))

    def attend(q, state):
        hi = state.astype(jnp.bfloat16)
        low = (state - hi.astype(jnp.float32)).astype(jnp.bfloat16)
        return dot(jnp.concatenate([q, q], axis=1), jnp.concatenate([hi, low], axis=0))

    def finish(base, g, a, inv):
        mean = jnp.sum(a * a, axis=-1, keepdims=True) * (1.0 / size)
        scale = inv * lax.rsqrt(mean * (inv * inv) + 1e-05)
        return (base.astype(jnp.float32) + g * a * scale).astype(jnp.bfloat16)

    total = jnp.zeros((toks, LANES), jnp.float32)
    for j in range(heads):
        mixed = finish(xh[j], gs[j], attend(qs[j], dot_t(ks[j], vs[j])), iv[...])
        xh[j] = mixed
        mf = mixed.astype(jnp.float32)
        total = total + mf * mf
    sq[r] = jnp.broadcast_to(jnp.sum(total, axis=-1, keepdims=True), (toks, LANES))

    swap_q = []
    for i, p in enumerate(rows_peers):
        c = pltpu.make_async_remote_copy(
            src_ref=sq.at[r], dst_ref=sq.at[r], send_sem=qsend.at[i], recv_sem=qrecv.at[i],
            device_id={"row": p}, device_id_type=MESH)
        c.start()
        swap_q.append(c)
    for j in range(heads):
        q, k, vv, g = project(xh[j], wj[1, j])
        qs[j] = q
        ks[j] = k
        vraw[j] = vv
        gs[j] = g
    for c in swap_q:
        c.wait_recv()
    inv_c = lax.rsqrt(jnp.sum(sq[...], axis=0) * (1.0 / width) + 1e-06)
    iv[...] = inv_c

    chunks = [(0, size)]

    def share(c, j, h):
        rows = pl.ds(*chunks[h])
        return pltpu.make_async_remote_copy(
            src_ref=mine.at[j, rows], dst_ref=sx.at[c, j, rows], send_sem=ssend.at[j, h],
            recv_sem=srecv.at[c, j, h], device_id=to_owner, device_id_type=MESH)

    def chain(j, h):
        rows = pl.ds(*chunks[h])
        return pltpu.make_async_remote_copy(
            src_ref=zout.at[j, rows], dst_ref=zin.at[j, rows], send_sem=zsend.at[j, h],
            recv_sem=zrecv.at[j, h], device_id={"frame": lax.rem(f + ncol, ncol * nz)}, device_id_type=MESH)

    def give(c, j, h):
        rows = pl.ds(*chunks[h])
        return pltpu.make_async_remote_copy(
            src_ref=pout.at[c, j, rows], dst_ref=pin.at[j, rows], send_sem=psend.at[c, j, h],
            recv_sem=precv.at[j, h], device_id=client(c), device_id_type=MESH)

    for j in range(heads):
        state = dot_t(ks[j], (vraw[j] * (inv_c * inv_c)).astype(jnp.bfloat16))
        mine[j] = state[:size].astype(jnp.bfloat16)

        @pl.when(at_home)
        def _():
            sx[x, j] = mine[j]

        @pl.when(jnp.logical_not(at_home))
        def _():
            for h in range(len(chunks)):
                share(x, j, h).start()
        own[j] = state

    @pl.when(owner)
    def _():
        for j in range(heads):
            for h in range(len(chunks)):
                rows = pl.ds(*chunks[h])
                for c in range(ncol):
                    @pl.when(away(c))
                    def _():
                        share(c, j, h).wait_recv()
                here = [sx[c, j, rows].astype(jnp.float32) for c in range(ncol)]

                @pl.when(down)
                def _():
                    chain(j, h).wait_recv()

                total = zin[j, rows].astype(jnp.float32)
                before = []
                for c in range(ncol):
                    before.append(total)
                    total = total + here[c]

                @pl.when(up)
                def _():
                    zout[j, rows] = total.astype(jnp.bfloat16)
                    chain(j, h).start()

                for c in range(ncol):
                    pout[c, j, rows] = before[c].astype(jnp.bfloat16)

                    @pl.when(away(c))
                    def _():
                        give(c, j, h).start()

    for j in range(heads):
        gs[j] = jax.nn.sigmoid(gs[j] * inv_c)
        vraw[j] = attend(qs[j], own[j])

    tail = jnp.zeros((LANES - size, LANES), jnp.bfloat16)
    for j in range(heads):
        @pl.when(at_home)
        def _():
            pin[j] = pout[x, j]

        @pl.when(jnp.logical_not(at_home))
        def _():
            for h in range(len(chunks)):
                give(x, j, h).wait_recv()

        a = vraw[j] + dot(qs[j], jnp.concatenate([pin[j], tail], axis=0))
        done = finish(xh[j], gs[j], a, iv[...])
        out[0, :, :, j * size:(j + 1) * size] = done[:, :size].reshape(out.shape[1:3] + (size,))

    for c in swap_x + swap_q:
        c.wait_send()

    @pl.when(jnp.logical_not(at_home))
    def _():
        for j in range(heads):
            for h in range(len(chunks)):
                share(x, j, h).wait_send()

    for c in range(ncol):
        @pl.when(jnp.logical_and(owner, away(c)))
        def _():
            for j in range(heads):
                for h in range(len(chunks)):
                    give(c, j, h).wait_send()

    @pl.when(up)
    def _():
        for j in range(heads):
            for h in range(len(chunks)):
                chain(j, h).wait_send()


def solution(mesh):
    nrow, count = mesh.shape["row"], mesh.shape["frame"]
    ncol = columns_of(mesh)
    nz = count // ncol

    def body(latents, spatial_weights, causal_weights):
        _, band, cols, width = latents.shape
        maps, all_heads, size, _ = spatial_weights.shape
        heads = all_heads // nrow
        toks = nrow * band * cols
        bf, f32 = jnp.bfloat16, jnp.float32
        dma = pltpu.SemaphoreType.DMA
        peers = max(nrow - 1, 1)
        return pl.pallas_call(
            functools.partial(kernel, nrow, ncol, nz),
            out_shape=jax.ShapeDtypeStruct((1, band * nrow, cols, width // nrow), bf),
            in_specs=[pl.BlockSpec(memory_space=pltpu.HBM)] * 3,
            out_specs=pl.BlockSpec(memory_space=pltpu.VMEM),
            scratch_shapes=[
                pltpu.VMEM((nrow, band, cols, width), bf),
                pltpu.VMEM((maps, heads, size, size), bf),
                pltpu.VMEM((maps, heads, size, size), bf),
                pltpu.VMEM((2, heads, size, maps * LANES), bf),
                pltpu.VMEM((heads, toks, LANES), bf),
                pltpu.VMEM((toks, LANES), f32),
                pltpu.VMEM((nrow, toks, LANES), f32),
                pltpu.VMEM((heads, size, LANES), bf),
                pltpu.VMEM((ncol, heads, size, LANES), bf),
                pltpu.VMEM((heads, size, LANES), bf),
                pltpu.VMEM((heads, size, LANES), bf),
                pltpu.VMEM((heads, size, LANES), bf),
                pltpu.VMEM((ncol, heads, size, LANES), bf),
                pltpu.VMEM((heads, toks, LANES), bf),
                pltpu.VMEM((heads, toks, LANES), bf),
                pltpu.VMEM((heads, toks, LANES), bf),
                pltpu.VMEM((heads, toks, LANES), f32),
                pltpu.VMEM((heads, toks, LANES), f32),
                pltpu.VMEM((heads, LANES, LANES), f32),
                dma((3,)),
                dma((peers,)), dma((peers,)),
                dma((peers,)), dma((peers,)),
                dma((heads, 2)), dma((ncol, heads, 2)),
                dma((heads, 2)), dma((heads, 2)),
                dma((ncol, heads, 2)), dma((heads, 2)),
            ],
            compiler_params=pltpu.CompilerParams(
                collective_id=0, has_side_effects=True, vmem_limit_bytes=55_000_000),
        )(latents, spatial_weights, causal_weights)

    in_specs = (P(("group", "frame"), "row", None, None), P(), P())
    out_specs = P(("group", "frame"), None, None, "row")
    return jax.shard_map(body, mesh=mesh, in_specs=in_specs, out_specs=out_specs, check_vma=False)
```

```python
import functools

import jax
import jax.numpy as jnp
from jax import lax
from jax.experimental import pallas as pl
from jax.experimental.pallas import tpu as pltpu
from jax.sharding import PartitionSpec as P

MESH = pl.DeviceIdType.MESH
LANES = 128


def columns_of(mesh):
    count = mesh.shape["frame"]
    line = mesh.devices.reshape(mesh.shape["group"], count, mesh.shape["row"])[0, :, 0]
    places = [getattr(d, "coords", None) for d in line]
    if any(p is None or len(p) < 3 for p in places):
        return 2 if count % 2 == 0 else 1
    cols = 1
    while cols < count and places[cols][2] == places[0][2]:
        cols += 1
    return cols if count % cols == 0 else 1


def dot(a, b):
    return jnp.dot(a, b, preferred_element_type=jnp.float32)


def dot_t(a, b):
    return lax.dot_general(a, b, (((0,), (0,)), ((), ())), preferred_element_type=jnp.float32)


def kernel(nrow, ncol, nz, lat, sw, cw, out, xall, wsv, wcv, wj, xh, iv, sq, mine, sx, zin, zout, pin, pout, qs, ks, vs, vraw, gs, own,
           lsem, xsend, xrecv, qsend, qrecv, ssend, srecv, zsend, zrecv, psend, precv):
    heads, toks, _ = xh.shape
    size = wsv.shape[2]
    width = heads * nrow * size
    part = toks // nrow
    r = lax.axis_index("row")
    f = lax.axis_index("frame")
    z, x = lax.div(f, ncol), lax.rem(f, ncol)

    rows_peers = [lax.rem(r + d, nrow) for d in range(1, nrow)]

    spread = ncol >= nrow
    my_col, my_row = lax.rem(r, ncol), (nrow - 1 if spread else r)
    at_home = jnp.logical_and(x == my_col, r == my_row)
    held = x if spread else r
    owner = jnp.logical_and(r == nrow - 1, x < nrow) if spread else x == my_col
    up, down = jnp.logical_and(owner, z < nz - 1), jnp.logical_and(owner, z > 0)
    to_owner = {"frame": z * ncol + my_col, "row": my_row}

    def client(c):
        return {"frame": z * ncol + c, "row": lax.rem(held, nrow)}

    def away(c):
        return jnp.logical_not(jnp.logical_and(held == r, c == x))

    barrier = pltpu.get_barrier_semaphore()
    for p in rows_peers:
        pl.semaphore_signal(barrier, inc=1, device_id={"row": p}, device_id_type=MESH)

    @pl.when(jnp.logical_not(at_home))
    def _():
        pl.semaphore_signal(barrier, inc=1, device_id=to_owner, device_id_type=MESH)

    for c in range(ncol):
        @pl.when(jnp.logical_and(owner, away(c)))
        def _():
            pl.semaphore_signal(barrier, inc=1, device_id=client(c), device_id_type=MESH)

    @pl.when(down)
    def _():
        pl.semaphore_signal(barrier, inc=1, device_id={"frame": f - ncol}, device_id_type=MESH)

    @pl.when(up)
    def _():
        pl.semaphore_signal(barrier, inc=1, device_id={"frame": f + ncol}, device_id_type=MESH)

    get_x = pltpu.make_async_copy(lat.at[0], xall.at[r], lsem.at[0])
    get_s = pltpu.make_async_copy(sw.at[:, pl.ds(r * heads, heads)], wsv, lsem.at[1])
    get_c = pltpu.make_async_copy(cw.at[:, pl.ds(r * heads, heads)], wcv, lsem.at[2])
    get_x.start()
    get_s.start()
    get_c.start()

    @pl.when(z == 0)
    def _():
        zin[...] = jnp.zeros_like(zin)

    pad = jnp.zeros((part, LANES - size), jnp.bfloat16)
    wpad = jnp.zeros((size, LANES - size), jnp.bfloat16)

    def join(w, j):
        return jnp.concatenate([t for k in range(4) for t in (w[k, j], wpad)], axis=1)

    def project(u, w):
        m = dot(u[:, :size], w)
        q = jnp.maximum(m[:, :LANES], 0.0).astype(jnp.bfloat16)
        k = jnp.maximum(m[:, LANES:2 * LANES], 0.0).astype(jnp.bfloat16)
        return q, k, m[:, 2 * LANES:3 * LANES], m[:, 3 * LANES:]

    def prepare(slot):
        rows = pl.ds(pl.multiple_of(slot * part, part), part)
        v = xall[slot].reshape(part, width)
        vf = v.astype(jnp.float32)
        inv = lax.rsqrt(jnp.sum(vf * vf, axis=-1, keepdims=True) * (1.0 / width) + 1e-06)
        iv[rows, :] = jnp.broadcast_to(inv, (part, LANES))
        for rr in range(nrow):
            @pl.when(r == rr)
            def _():
                for j in range(heads):
                    lo = (rr * heads + j) * size
                    xh[j, rows, :] = jnp.concatenate([v[:, lo:lo + size], pad], axis=1)

    def maps(slot):
        rows = pl.ds(pl.multiple_of(slot * part, part), part)
        inv = iv[rows, :]
        for j in range(heads):
            q, k, vv, g = project(xh[j, rows, :], wj[0, j])
            qs[j, rows, :] = q
            ks[j, rows, :] = k
            vs[j, rows, :] = (vv * (inv * inv)).astype(jnp.bfloat16)
            gs[j, rows, :] = jax.nn.sigmoid(g * inv)

    get_x.wait()
    prepare(r)
    get_s.wait()
    for j in range(heads):
        wj[0, j] = join(wsv, j)

    ends = jnp.where(z > 0, 1, 0) + jnp.where(z < nz - 1, 1, 0)
    clients = ncol - jnp.where(held == r, 1, 0)
    pl.semaphore_wait(barrier, (nrow - 1) + jnp.where(at_home, 0, 1) + jnp.where(owner, clients + ends, 0))

    swap_x = []
    for i, p in enumerate(rows_peers):
        c = pltpu.make_async_remote_copy(
            src_ref=lat.at[0], dst_ref=xall.at[r], send_sem=xsend.at[i], recv_sem=xrecv.at[i],
            device_id={"row": p}, device_id_type=MESH)
        c.start()
        swap_x.append(c)

    maps(r)
    get_c.wait()
    for j in range(heads):
        wj[1, j] = join(wcv, j)
    for i, c in enumerate(swap_x):
        c.wait_recv()
        prepare(lax.rem(r + (nrow - 1 - i), nrow))
        maps(lax.rem(r + (nrow - 1 - i), nrow))

    def attend(q, state):
        hi = state.astype(jnp.bfloat16)
        low = (state - hi.astype(jnp.float32)).astype(jnp.bfloat16)
        return dot(jnp.concatenate([q, q], axis=1), jnp.concatenate([hi, low], axis=0))

    def finish(base, g, a, inv):
        mean = jnp.sum(a * a, axis=-1, keepdims=True) * (1.0 / size)
        scale = inv * lax.rsqrt(mean * (inv * inv) + 1e-05)
        return (base.astype(jnp.float32) + g * a * scale).astype(jnp.bfloat16)

    total = jnp.zeros((toks, LANES), jnp.float32)
    for j in range(heads):
        mixed = finish(xh[j], gs[j], attend(qs[j], dot_t(ks[j], vs[j])), iv[...])
        xh[j] = mixed
        mf = mixed.astype(jnp.float32)
        total = total + mf * mf
    sq[r] = jnp.broadcast_to(jnp.sum(total, axis=-1, keepdims=True), (toks, LANES))

    swap_q = []
    for i, p in enumerate(rows_peers):
        c = pltpu.make_async_remote_copy(
            src_ref=sq.at[r], dst_ref=sq.at[r], send_sem=qsend.at[i], recv_sem=qrecv.at[i],
            device_id={"row": p}, device_id_type=MESH)
        c.start()
        swap_q.append(c)
    for j in range(heads):
        q, k, vv, g = project(xh[j], wj[1, j])
        qs[j] = q
        ks[j] = k
        vraw[j] = vv
        gs[j] = g
    for c in swap_q:
        c.wait_recv()
    inv_c = lax.rsqrt(jnp.sum(sq[...], axis=0) * (1.0 / width) + 1e-06)
    iv[...] = inv_c

    tiles, pieces = size // 16, zsend.shape[1]
    edges = [16 * ((tiles * i + pieces - 1) // pieces) for i in range(pieces)] + [size]
    chunks = [(a, b - a) for a, b in zip(edges[:-1], edges[1:])]

    def share(c, j, h):
        rows = pl.ds(*chunks[h])
        return pltpu.make_async_remote_copy(
            src_ref=mine.at[j, rows], dst_ref=sx.at[c, j, rows], send_sem=ssend.at[j, h],
            recv_sem=srecv.at[c, j, h], device_id=to_owner, device_id_type=MESH)

    def chain(j, h):
        rows = pl.ds(*chunks[h])
        return pltpu.make_async_remote_copy(
            src_ref=zout.at[j, rows], dst_ref=zin.at[j, rows], send_sem=zsend.at[j, h],
            recv_sem=zrecv.at[j, h], device_id={"frame": lax.rem(f + ncol, ncol * nz)}, device_id_type=MESH)

    def give(c, j, h):
        rows = pl.ds(*chunks[h])
        return pltpu.make_async_remote_copy(
            src_ref=pout.at[c, j, rows], dst_ref=pin.at[j, rows], send_sem=psend.at[c, j, h],
            recv_sem=precv.at[j, h], device_id=client(c), device_id_type=MESH)

    for j in range(heads):
        state = dot_t(ks[j], (vraw[j] * (inv_c * inv_c)).astype(jnp.bfloat16))
        mine[j] = state[:size].astype(jnp.bfloat16)

        @pl.when(at_home)
        def _():
            sx[x, j] = mine[j]

        @pl.when(jnp.logical_not(at_home))
        def _():
            for h in range(len(chunks)):
                share(x, j, h).start()
        own[j] = state

    @pl.when(owner)
    def _():
        for j in range(heads):
            for h in range(len(chunks)):
                rows = pl.ds(*chunks[h])
                for c in range(ncol):
                    @pl.when(away(c))
                    def _():
                        share(c, j, h).wait_recv()
                here = [sx[c, j, rows].astype(jnp.float32) for c in range(ncol)]

                @pl.when(down)
                def _():
                    chain(j, h).wait_recv()

                total = zin[j, rows].astype(jnp.float32)
                before = []
                for c in range(ncol):
                    before.append(total)
                    total = total + here[c]

                @pl.when(up)
                def _():
                    zout[j, rows] = total.astype(jnp.bfloat16)
                    chain(j, h).start()

                for c in range(ncol):
                    pout[c, j, rows] = before[c].astype(jnp.bfloat16)

                    @pl.when(away(c))
                    def _():
                        give(c, j, h).start()

    for j in range(heads):
        gs[j] = jax.nn.sigmoid(gs[j] * inv_c)
        vraw[j] = attend(qs[j], own[j])

    tail = jnp.zeros((LANES - size, LANES), jnp.bfloat16)
    def complete(j):
        a = vraw[j] + dot(qs[j], jnp.concatenate([pin[j], tail], axis=0))
        done = finish(xh[j], gs[j], a, iv[...])
        out[0, :, :, j * size:(j + 1) * size] = done[:, :size].reshape(out.shape[1:3] + (size,))

    @pl.when(owner)
    def _():
        @pl.when(at_home)
        def _():
            for j in range(heads):
                pin[j] = pout[x, j]

        @pl.when(jnp.logical_not(at_home))
        def _():
            for j in range(heads):
                for h in range(len(chunks)):
                    give(x, j, h).wait_recv()

        for j in range(heads):
            complete(j)

    @pl.when(jnp.logical_not(owner))
    def _():
        for j in range(heads):
            for h in range(len(chunks)):
                give(x, j, h).wait_recv()
            complete(j)

    for c in swap_x + swap_q:
        c.wait_send()

    @pl.when(jnp.logical_not(at_home))
    def _():
        for j in range(heads):
            for h in range(len(chunks)):
                share(x, j, h).wait_send()

    for c in range(ncol):
        @pl.when(jnp.logical_and(owner, away(c)))
        def _():
            for j in range(heads):
                for h in range(len(chunks)):
                    give(c, j, h).wait_send()

    @pl.when(up)
    def _():
        for j in range(heads):
            for h in range(len(chunks)):
                chain(j, h).wait_send()


def solution(mesh):
    nrow, count = mesh.shape["row"], mesh.shape["frame"]
    ncol = columns_of(mesh)
    nz = count // ncol

    def body(latents, spatial_weights, causal_weights):
        _, band, cols, width = latents.shape
        maps, all_heads, size, _ = spatial_weights.shape
        heads = all_heads // nrow
        toks = nrow * band * cols
        bf, f32 = jnp.bfloat16, jnp.float32
        dma = pltpu.SemaphoreType.DMA
        peers, pieces = max(nrow - 1, 1), min(3, size // 16)
        return pl.pallas_call(
            functools.partial(kernel, nrow, ncol, nz),
            out_shape=jax.ShapeDtypeStruct((1, band * nrow, cols, width // nrow), bf),
            in_specs=[pl.BlockSpec(memory_space=pltpu.HBM)] * 3,
            out_specs=pl.BlockSpec(memory_space=pltpu.VMEM),
            scratch_shapes=[
                pltpu.VMEM((nrow, band, cols, width), bf),
                pltpu.VMEM((maps, heads, size, size), bf),
                pltpu.VMEM((maps, heads, size, size), bf),
                pltpu.VMEM((2, heads, size, maps * LANES), bf),
                pltpu.VMEM((heads, toks, LANES), bf),
                pltpu.VMEM((toks, LANES), f32),
                pltpu.VMEM((nrow, toks, LANES), f32),
                pltpu.VMEM((heads, size, LANES), bf),
                pltpu.VMEM((ncol, heads, size, LANES), bf),
                pltpu.VMEM((heads, size, LANES), bf),
                pltpu.VMEM((heads, size, LANES), bf),
                pltpu.VMEM((heads, size, LANES), bf),
                pltpu.VMEM((ncol, heads, size, LANES), bf),
                pltpu.VMEM((heads, toks, LANES), bf),
                pltpu.VMEM((heads, toks, LANES), bf),
                pltpu.VMEM((heads, toks, LANES), bf),
                pltpu.VMEM((heads, toks, LANES), f32),
                pltpu.VMEM((heads, toks, LANES), f32),
                pltpu.VMEM((heads, LANES, LANES), f32),
                dma((3,)),
                dma((peers,)), dma((peers,)),
                dma((peers,)), dma((peers,)),
                dma((heads, pieces)), dma((ncol, heads, pieces)),
                dma((heads, pieces)), dma((heads, pieces)),
                dma((ncol, heads, pieces)), dma((heads, pieces)),
            ],
            compiler_params=pltpu.CompilerParams(
                collective_id=0, has_side_effects=True, vmem_limit_bytes=55_000_000),
        )(latents, spatial_weights, causal_weights)

    in_specs = (P(("group", "frame"), "row", None, None), P(), P())
    out_specs = P(("group", "frame"), None, None, "row")
    return jax.shard_map(body, mesh=mesh, in_specs=in_specs, out_specs=out_specs, check_vma=False)
```

```python
import functools

import jax
import jax.numpy as jnp
from jax import lax
from jax.experimental import pallas as pl
from jax.experimental.pallas import tpu as pltpu
from jax.sharding import PartitionSpec as P

MESH = pl.DeviceIdType.MESH
LANES = 128


def columns_of(mesh):
    count = mesh.shape["frame"]
    line = mesh.devices.reshape(mesh.shape["group"], count, mesh.shape["row"])[0, :, 0]
    places = [getattr(d, "coords", None) for d in line]
    if any(p is None or len(p) < 3 for p in places):
        return 2 if count % 2 == 0 else 1
    cols = 1
    while cols < count and places[cols][2] == places[0][2]:
        cols += 1
    return cols if count % cols == 0 else 1


def dot(a, b):
    return jnp.dot(a, b, preferred_element_type=jnp.float32)


def dot_t(a, b):
    return lax.dot_general(a, b, (((0,), (0,)), ((), ())), preferred_element_type=jnp.float32)


def kernel(nrow, ncol, nz, lat, sw, cw, out, xall, wsv, wcv, wj, xh, iv, sq, mine, sx, zin, zout, pin, pout, qs, ks, vs, vraw, gs, own,
           lsem, xsend, xrecv, qsend, qrecv, ssend, srecv, zsend, zrecv, psend, precv):
    heads, toks, _ = xh.shape
    size = wsv.shape[2]
    width = heads * nrow * size
    part = toks // nrow
    r = lax.axis_index("row")
    f = lax.axis_index("frame")
    z, x = lax.div(f, ncol), lax.rem(f, ncol)

    rows_peers = [lax.rem(r + d, nrow) for d in range(1, nrow)]

    spread = ncol >= nrow
    my_col, my_row = lax.rem(r, ncol), (nrow - 1 if spread else r)
    at_home = jnp.logical_and(x == my_col, r == my_row)
    held = x if spread else r
    owner = jnp.logical_and(r == nrow - 1, x < nrow) if spread else x == my_col
    up, down = jnp.logical_and(owner, z < nz - 1), jnp.logical_and(owner, z > 0)
    to_owner = {"frame": z * ncol + my_col, "row": my_row}

    def client(c):
        return {"frame": z * ncol + c, "row": lax.rem(held, nrow)}

    def away(c):
        return jnp.logical_not(jnp.logical_and(held == r, c == x))

    barrier = pltpu.get_barrier_semaphore()
    for p in rows_peers:
        pl.semaphore_signal(barrier, inc=1, device_id={"row": p}, device_id_type=MESH)

    @pl.when(jnp.logical_not(at_home))
    def _():
        pl.semaphore_signal(barrier, inc=1, device_id=to_owner, device_id_type=MESH)

    for c in range(ncol):
        @pl.when(jnp.logical_and(owner, away(c)))
        def _():
            pl.semaphore_signal(barrier, inc=1, device_id=client(c), device_id_type=MESH)

    @pl.when(down)
    def _():
        pl.semaphore_signal(barrier, inc=1, device_id={"frame": f - ncol}, device_id_type=MESH)

    @pl.when(up)
    def _():
        pl.semaphore_signal(barrier, inc=1, device_id={"frame": f + ncol}, device_id_type=MESH)

    get_x = pltpu.make_async_copy(lat.at[0], xall.at[r], lsem.at[0])
    get_s = pltpu.make_async_copy(sw.at[:, pl.ds(r * heads, heads)], wsv, lsem.at[1])
    get_c = pltpu.make_async_copy(cw.at[:, pl.ds(r * heads, heads)], wcv, lsem.at[2])
    get_x.start()
    get_s.start()
    get_c.start()

    @pl.when(z == 0)
    def _():
        zin[...] = jnp.zeros_like(zin)

    ends = jnp.where(z > 0, 1, 0) + jnp.where(z < nz - 1, 1, 0)
    clients = ncol - jnp.where(held == r, 1, 0)
    pl.semaphore_wait(barrier, (nrow - 1) + jnp.where(at_home, 0, 1) + jnp.where(owner, clients + ends, 0))

    swap_x = []
    for i, p in enumerate(rows_peers):
        c = pltpu.make_async_remote_copy(
            src_ref=lat.at[0], dst_ref=xall.at[r], send_sem=xsend.at[i], recv_sem=xrecv.at[i],
            device_id={"row": p}, device_id_type=MESH)
        c.start()
        swap_x.append(c)

    pad = jnp.zeros((part, LANES - size), jnp.bfloat16)
    wpad = jnp.zeros((size, LANES - size), jnp.bfloat16)

    def join(w, j):
        return jnp.concatenate([t for k in range(4) for t in (w[k, j], wpad)], axis=1)

    def project(u, w):
        m = dot(u[:, :size], w)
        q = jnp.maximum(m[:, :LANES], 0.0).astype(jnp.bfloat16)
        k = jnp.maximum(m[:, LANES:2 * LANES], 0.0).astype(jnp.bfloat16)
        return q, k, m[:, 2 * LANES:3 * LANES], m[:, 3 * LANES:]

    def stage(slot):
        rows = pl.ds(pl.multiple_of(slot * part, part), part)
        v = xall[slot].reshape(part, width)
        vf = v.astype(jnp.float32)
        inv = lax.rsqrt(jnp.sum(vf * vf, axis=-1, keepdims=True) * (1.0 / width) + 1e-06)
        inv = jnp.broadcast_to(inv, (part, LANES))
        iv[rows, :] = inv
        for rr in range(nrow):
            @pl.when(r == rr)
            def _():
                for j in range(heads):
                    lo = (rr * heads + j) * size
                    xh[j, rows, :] = jnp.concatenate([v[:, lo:lo + size], pad], axis=1)
        for j in range(heads):
            q, k, vv, g = project(xh[j, rows, :], wj[j])
            qs[j, rows, :] = q
            ks[j, rows, :] = k
            vs[j, rows, :] = (vv * (inv * inv)).astype(jnp.bfloat16)
            gs[j, rows, :] = jax.nn.sigmoid(g * inv)

    get_s.wait()
    for j in range(heads):
        wj[j] = join(wsv, j)
    get_x.wait()
    stage(r)
    for i, c in enumerate(swap_x):
        c.wait_recv()
        stage(lax.rem(r + (nrow - 1 - i), nrow))

    def attend(q, state):
        hi = state.astype(jnp.bfloat16)
        low = (state - hi.astype(jnp.float32)).astype(jnp.bfloat16)
        return dot(jnp.concatenate([q, q], axis=1), jnp.concatenate([hi, low], axis=0))

    def finish(base, g, a, inv):
        mean = jnp.sum(a * a, axis=-1, keepdims=True) * (1.0 / size)
        scale = inv * lax.rsqrt(mean * (inv * inv) + 1e-05)
        return (base.astype(jnp.float32) + g * a * scale).astype(jnp.bfloat16)

    total = jnp.zeros((toks, LANES), jnp.float32)
    for j in range(heads):
        mixed = finish(xh[j], gs[j], attend(qs[j], dot_t(ks[j], vs[j])), iv[...])
        xh[j] = mixed
        mf = mixed.astype(jnp.float32)
        total = total + mf * mf
    sq[r] = jnp.broadcast_to(jnp.sum(total, axis=-1, keepdims=True), (toks, LANES))

    swap_q = []
    for i, p in enumerate(rows_peers):
        c = pltpu.make_async_remote_copy(
            src_ref=sq.at[r], dst_ref=sq.at[r], send_sem=qsend.at[i], recv_sem=qrecv.at[i],
            device_id={"row": p}, device_id_type=MESH)
        c.start()
        swap_q.append(c)
    get_c.wait()
    for j in range(heads):
        q, k, vv, g = project(xh[j], join(wcv, j))
        qs[j] = q
        ks[j] = k
        vraw[j] = vv
        gs[j] = g
    for c in swap_q:
        c.wait_recv()
    inv_c = lax.rsqrt(jnp.sum(sq[...], axis=0) * (1.0 / width) + 1e-06)
    iv[...] = inv_c

    cut = (size // 2 + 15) // 16 * 16
    chunks = [(0, cut), (cut, size - cut)]

    def share(c, j, h):
        rows = pl.ds(*chunks[h])
        return pltpu.make_async_remote_copy(
            src_ref=mine.at[j, rows], dst_ref=sx.at[c, j, rows], send_sem=ssend.at[j, h],
            recv_sem=srecv.at[c, j, h], device_id=to_owner, device_id_type=MESH)

    def chain(j, h):
        rows = pl.ds(*chunks[h])
        return pltpu.make_async_remote_copy(
            src_ref=zout.at[j, rows], dst_ref=zin.at[j, rows], send_sem=zsend.at[j, h],
            recv_sem=zrecv.at[j, h], device_id={"frame": lax.rem(f + ncol, ncol * nz)}, device_id_type=MESH)

    def give(c, j, h):
        rows = pl.ds(*chunks[h])
        return pltpu.make_async_remote_copy(
            src_ref=pout.at[c, j, rows], dst_ref=pin.at[j, rows], send_sem=psend.at[c, j, h],
            recv_sem=precv.at[j, h], device_id=client(c), device_id_type=MESH)

    for j in range(heads):
        state = dot_t(ks[j], (vraw[j] * (inv_c * inv_c)).astype(jnp.bfloat16))
        mine[j] = state[:size].astype(jnp.bfloat16)

        @pl.when(at_home)
        def _():
            sx[x, j] = mine[j]

        @pl.when(jnp.logical_not(at_home))
        def _():
            for h in range(2):
                share(x, j, h).start()
        own[j] = state

    for j in range(heads):
        gs[j] = jax.nn.sigmoid(gs[j] * inv_c)
        vraw[j] = attend(qs[j], own[j])

    @pl.when(owner)
    def _():
        for j in range(heads):
            for h in range(2):
                rows = pl.ds(*chunks[h])
                for c in range(ncol):
                    @pl.when(away(c))
                    def _():
                        share(c, j, h).wait_recv()
                here = [sx[c, j, rows].astype(jnp.float32) for c in range(ncol)]

                @pl.when(down)
                def _():
                    chain(j, h).wait_recv()

                total = zin[j, rows].astype(jnp.float32)
                before = []
                for c in range(ncol):
                    before.append(total)
                    total = total + here[c]

                @pl.when(up)
                def _():
                    zout[j, rows] = total.astype(jnp.bfloat16)
                    chain(j, h).start()

                for c in range(ncol):
                    pout[c, j, rows] = before[c].astype(jnp.bfloat16)

                    @pl.when(away(c))
                    def _():
                        give(c, j, h).start()

    tail = jnp.zeros((LANES - size, LANES), jnp.bfloat16)
    def complete(j):
        a = vraw[j] + dot(qs[j], jnp.concatenate([pin[j], tail], axis=0))
        done = finish(xh[j], gs[j], a, iv[...])
        out[0, :, :, j * size:(j + 1) * size] = done[:, :size].reshape(out.shape[1:3] + (size,))

    @pl.when(owner)
    def _():
        @pl.when(at_home)
        def _():
            for j in range(heads):
                pin[j] = pout[x, j]

        @pl.when(jnp.logical_not(at_home))
        def _():
            for j in range(heads):
                for h in range(2):
                    give(x, j, h).wait_recv()

        for j in range(heads):
            complete(j)

    @pl.when(jnp.logical_not(owner))
    def _():
        for j in range(heads):
            for h in range(2):
                give(x, j, h).wait_recv()
            complete(j)

    for c in swap_x + swap_q:
        c.wait_send()

    @pl.when(jnp.logical_not(at_home))
    def _():
        for j in range(heads):
            for h in range(2):
                share(x, j, h).wait_send()

    for c in range(ncol):
        @pl.when(jnp.logical_and(owner, away(c)))
        def _():
            for j in range(heads):
                for h in range(2):
                    give(c, j, h).wait_send()

    @pl.when(up)
    def _():
        for j in range(heads):
            for h in range(2):
                chain(j, h).wait_send()


def solution(mesh):
    nrow, count = mesh.shape["row"], mesh.shape["frame"]
    ncol = columns_of(mesh)
    nz = count // ncol

    def body(latents, spatial_weights, causal_weights):
        _, band, cols, width = latents.shape
        maps, all_heads, size, _ = spatial_weights.shape
        heads = all_heads // nrow
        toks = nrow * band * cols
        bf, f32 = jnp.bfloat16, jnp.float32
        dma = pltpu.SemaphoreType.DMA
        peers = max(nrow - 1, 1)
        return pl.pallas_call(
            functools.partial(kernel, nrow, ncol, nz),
            out_shape=jax.ShapeDtypeStruct((1, band * nrow, cols, width // nrow), bf),
            in_specs=[pl.BlockSpec(memory_space=pltpu.HBM)] * 3,
            out_specs=pl.BlockSpec(memory_space=pltpu.VMEM),
            scratch_shapes=[
                pltpu.VMEM((nrow, band, cols, width), bf),
                pltpu.VMEM((maps, heads, size, size), bf),
                pltpu.VMEM((maps, heads, size, size), bf),
                pltpu.VMEM((heads, size, maps * LANES), bf),
                pltpu.VMEM((heads, toks, LANES), bf),
                pltpu.VMEM((toks, LANES), f32),
                pltpu.VMEM((nrow, toks, LANES), f32),
                pltpu.VMEM((heads, size, LANES), bf),
                pltpu.VMEM((ncol, heads, size, LANES), bf),
                pltpu.VMEM((heads, size, LANES), bf),
                pltpu.VMEM((heads, size, LANES), bf),
                pltpu.VMEM((heads, size, LANES), bf),
                pltpu.VMEM((ncol, heads, size, LANES), bf),
                pltpu.VMEM((heads, toks, LANES), bf),
                pltpu.VMEM((heads, toks, LANES), bf),
                pltpu.VMEM((heads, toks, LANES), bf),
                pltpu.VMEM((heads, toks, LANES), f32),
                pltpu.VMEM((heads, toks, LANES), f32),
                pltpu.VMEM((heads, LANES, LANES), f32),
                dma((3,)),
                dma((peers,)), dma((peers,)),
                dma((peers,)), dma((peers,)),
                dma((heads, 2)), dma((ncol, heads, 2)),
                dma((heads, 2)), dma((heads, 2)),
                dma((ncol, heads, 2)), dma((heads, 2)),
            ],
            compiler_params=pltpu.CompilerParams(
                collective_id=0, has_side_effects=True, vmem_limit_bytes=55_000_000),
        )(latents, spatial_weights, causal_weights)

    in_specs = (P(("group", "frame"), "row", None, None), P(), P())
    out_specs = P(("group", "frame"), None, None, "row")
    return jax.shard_map(body, mesh=mesh, in_specs=in_specs, out_specs=out_specs, check_vma=False)
```

```python
import functools

import jax
import jax.numpy as jnp
from jax import lax
from jax.experimental import pallas as pl
from jax.experimental.pallas import tpu as pltpu
from jax.sharding import PartitionSpec as P

MESH = pl.DeviceIdType.MESH
LANES = 128


def columns_of(mesh):
    count = mesh.shape["frame"]
    line = mesh.devices.reshape(mesh.shape["group"], count, mesh.shape["row"])[0, :, 0]
    places = [getattr(d, "coords", None) for d in line]
    if any(p is None or len(p) < 3 for p in places):
        return 2 if count % 2 == 0 else 1
    cols = 1
    while cols < count and places[cols][2] == places[0][2]:
        cols += 1
    return cols if count % cols == 0 else 1


def dot(a, b):
    return jnp.dot(a, b, preferred_element_type=jnp.float32)


def dot_t(a, b):
    return lax.dot_general(a, b, (((0,), (0,)), ((), ())), preferred_element_type=jnp.float32)


def kernel(nrow, ncol, nz, lat, sw, cw, out, xall, wsv, wcv, wj, xh, iv, sq, mine, sx, zin, zout, pin, pout, qs, ks, vs, vraw, gs, own,
           lsem, xsend, xrecv, qsend, qrecv, ssend, srecv, zsend, zrecv, psend, precv):
    heads, toks, _ = xh.shape
    size = wsv.shape[2]
    width = heads * nrow * size
    part = toks // nrow
    r = lax.axis_index("row")
    f = lax.axis_index("frame")
    z, x = lax.div(f, ncol), lax.rem(f, ncol)

    rows_peers = [lax.rem(r + d, nrow) for d in range(1, nrow)]

    spread = ncol >= nrow
    my_col, my_row = lax.rem(r, ncol), (nrow - 1 if spread else r)
    at_home = jnp.logical_and(x == my_col, r == my_row)
    held = x if spread else r
    owner = jnp.logical_and(r == nrow - 1, x < nrow) if spread else x == my_col
    up, down = jnp.logical_and(owner, z < nz - 1), jnp.logical_and(owner, z > 0)
    to_owner = {"frame": z * ncol + my_col, "row": my_row}

    def client(c):
        return {"frame": z * ncol + c, "row": lax.rem(held, nrow)}

    def away(c):
        return jnp.logical_not(jnp.logical_and(held == r, c == x))

    barrier = pltpu.get_barrier_semaphore()
    for p in rows_peers:
        pl.semaphore_signal(barrier, inc=1, device_id={"row": p}, device_id_type=MESH)

    @pl.when(jnp.logical_not(at_home))
    def _():
        pl.semaphore_signal(barrier, inc=1, device_id=to_owner, device_id_type=MESH)

    for c in range(ncol):
        @pl.when(jnp.logical_and(owner, away(c)))
        def _():
            pl.semaphore_signal(barrier, inc=1, device_id=client(c), device_id_type=MESH)

    @pl.when(down)
    def _():
        pl.semaphore_signal(barrier, inc=1, device_id={"frame": f - ncol}, device_id_type=MESH)

    @pl.when(up)
    def _():
        pl.semaphore_signal(barrier, inc=1, device_id={"frame": f + ncol}, device_id_type=MESH)

    get_x = pltpu.make_async_copy(lat.at[0], xall.at[r], lsem.at[0])
    get_s = pltpu.make_async_copy(sw.at[:, pl.ds(r * heads, heads)], wsv, lsem.at[1])
    get_c = pltpu.make_async_copy(cw.at[:, pl.ds(r * heads, heads)], wcv, lsem.at[2])
    get_x.start()
    get_s.start()
    get_c.start()

    @pl.when(z == 0)
    def _():
        zin[...] = jnp.zeros_like(zin)

    ends = jnp.where(z > 0, 1, 0) + jnp.where(z < nz - 1, 1, 0)
    clients = ncol - jnp.where(held == r, 1, 0)
    pl.semaphore_wait(barrier, (nrow - 1) + jnp.where(at_home, 0, 1) + jnp.where(owner, clients + ends, 0))

    swap_x = []
    for i, p in enumerate(rows_peers):
        c = pltpu.make_async_remote_copy(
            src_ref=lat.at[0], dst_ref=xall.at[r], send_sem=xsend.at[i], recv_sem=xrecv.at[i],
            device_id={"row": p}, device_id_type=MESH)
        c.start()
        swap_x.append(c)

    pad = jnp.zeros((part, LANES - size), jnp.bfloat16)
    wpad = jnp.zeros((size, LANES - size), jnp.bfloat16)

    def join(w, j):
        return jnp.concatenate([t for k in range(4) for t in (w[k, j], wpad)], axis=1)

    def project(u, w):
        m = dot(u[:, :size], w)
        q = jnp.maximum(m[:, :LANES], 0.0).astype(jnp.bfloat16)
        k = jnp.maximum(m[:, LANES:2 * LANES], 0.0).astype(jnp.bfloat16)
        return q, k, m[:, 2 * LANES:3 * LANES], m[:, 3 * LANES:]

    def stage(slot):
        rows = pl.ds(pl.multiple_of(slot * part, part), part)
        v = xall[slot].reshape(part, width)
        vf = v.astype(jnp.float32)
        inv = lax.rsqrt(jnp.sum(vf * vf, axis=-1, keepdims=True) * (1.0 / width) + 1e-06)
        inv = jnp.broadcast_to(inv, (part, LANES))
        iv[rows, :] = inv
        for rr in range(nrow):
            @pl.when(r == rr)
            def _():
                for j in range(heads):
                    lo = (rr * heads + j) * size
                    xh[j, rows, :] = jnp.concatenate([v[:, lo:lo + size], pad], axis=1)
        for j in range(heads):
            q, k, vv, g = project(xh[j, rows, :], wj[j])
            qs[j, rows, :] = q
            ks[j, rows, :] = k
            vs[j, rows, :] = (vv * (inv * inv)).astype(jnp.bfloat16)
            gs[j, rows, :] = jax.nn.sigmoid(g * inv)

    get_s.wait()
    for j in range(heads):
        wj[j] = join(wsv, j)
    get_x.wait()
    stage(r)
    for i, c in enumerate(swap_x):
        c.wait_recv()
        stage(lax.rem(r + (nrow - 1 - i), nrow))

    def attend(q, state):
        hi = state.astype(jnp.bfloat16)
        low = (state - hi.astype(jnp.float32)).astype(jnp.bfloat16)
        return dot(jnp.concatenate([q, q], axis=1), jnp.concatenate([hi, low], axis=0))

    def finish(base, g, a, inv):
        mean = jnp.sum(a * a, axis=-1, keepdims=True) * (1.0 / size)
        scale = inv * lax.rsqrt(mean * (inv * inv) + 1e-05)
        return (base.astype(jnp.float32) + g * a * scale).astype(jnp.bfloat16)

    total = jnp.zeros((toks, LANES), jnp.float32)
    for j in range(heads):
        mixed = finish(xh[j], gs[j], attend(qs[j], dot_t(ks[j], vs[j])), iv[...])
        xh[j] = mixed
        mf = mixed.astype(jnp.float32)
        total = total + mf * mf
    sq[r] = jnp.broadcast_to(jnp.sum(total, axis=-1, keepdims=True), (toks, LANES))

    swap_q = []
    for i, p in enumerate(rows_peers):
        c = pltpu.make_async_remote_copy(
            src_ref=sq.at[r], dst_ref=sq.at[r], send_sem=qsend.at[i], recv_sem=qrecv.at[i],
            device_id={"row": p}, device_id_type=MESH)
        c.start()
        swap_q.append(c)
    get_c.wait()
    for j in range(heads):
        q, k, vv, g = project(xh[j], join(wcv, j))
        qs[j] = q
        ks[j] = k
        vraw[j] = vv
        gs[j] = g
    for c in swap_q:
        c.wait_recv()
    inv_c = lax.rsqrt(jnp.sum(sq[...], axis=0) * (1.0 / width) + 1e-06)
    iv[...] = inv_c

    cut = (size // 2 + 15) // 16 * 16
    chunks = [(0, cut), (cut, size - cut)]

    def share(c, j, h):
        rows = pl.ds(*chunks[h])
        return pltpu.make_async_remote_copy(
            src_ref=mine.at[j, rows], dst_ref=sx.at[c, j, rows], send_sem=ssend.at[j, h],
            recv_sem=srecv.at[c, j, h], device_id=to_owner, device_id_type=MESH)

    def chain(j, h):
        rows = pl.ds(*chunks[h])
        return pltpu.make_async_remote_copy(
            src_ref=zout.at[j, rows], dst_ref=zin.at[j, rows], send_sem=zsend.at[j, h],
            recv_sem=zrecv.at[j, h], device_id={"frame": lax.rem(f + ncol, ncol * nz)}, device_id_type=MESH)

    def give(c, j, h):
        rows = pl.ds(*chunks[h])
        return pltpu.make_async_remote_copy(
            src_ref=pout.at[c, j, rows], dst_ref=pin.at[j, rows], send_sem=psend.at[c, j, h],
            recv_sem=precv.at[j, h], device_id=client(c), device_id_type=MESH)

    for j in range(heads):
        state = dot_t(ks[j], (vraw[j] * (inv_c * inv_c)).astype(jnp.bfloat16))
        mine[j] = state[:size].astype(jnp.bfloat16)

        @pl.when(at_home)
        def _():
            sx[x, j] = mine[j]

        @pl.when(jnp.logical_not(at_home))
        def _():
            for h in range(2):
                share(x, j, h).start()
        own[j] = state

    for j in range(heads):
        gs[j] = jax.nn.sigmoid(gs[j] * inv_c)
        vraw[j] = attend(qs[j], own[j])

    tail = jnp.zeros((LANES - size, LANES), jnp.bfloat16)
    mixing = jnp.logical_and(z == nz - 1, jnp.logical_not(at_home))

    def arrived(j):
        for h in range(2):
            give(x, j, h).wait_recv()

    def complete(j):
        a = vraw[j] + dot(qs[j], jnp.concatenate([pin[j], tail], axis=0))
        done = finish(xh[j], gs[j], a, iv[...])
        out[0, :, :, j * size:(j + 1) * size] = done[:, :size].reshape(out.shape[1:3] + (size,))

    @pl.when(owner)
    def _():
        for j in range(heads):
            if j > 1:
                @pl.when(mixing)
                def _():
                    arrived(j - 2)
                    complete(j - 2)

            for h in range(2):
                rows = pl.ds(*chunks[h])
                for c in range(ncol):
                    @pl.when(away(c))
                    def _():
                        share(c, j, h).wait_recv()
                here = [sx[c, j, rows].astype(jnp.float32) for c in range(ncol)]

                @pl.when(down)
                def _():
                    chain(j, h).wait_recv()

                total = zin[j, rows].astype(jnp.float32)
                before = []
                for c in range(ncol):
                    before.append(total)
                    total = total + here[c]

                @pl.when(up)
                def _():
                    zout[j, rows] = total.astype(jnp.bfloat16)
                    chain(j, h).start()

                for c in range(ncol):
                    pout[c, j, rows] = before[c].astype(jnp.bfloat16)

                    @pl.when(away(c))
                    def _():
                        give(c, j, h).start()

    @pl.when(owner)
    def _():
        @pl.when(at_home)
        def _():
            for j in range(heads):
                pin[j] = pout[x, j]

        @pl.when(mixing)
        def _():
            for j in range(max(heads - 2, 0), heads):
                arrived(j)
            for j in range(max(heads - 2, 0), heads):
                complete(j)

        @pl.when(jnp.logical_not(mixing))
        def _():
            @pl.when(jnp.logical_not(at_home))
            def _():
                for j in range(heads):
                    arrived(j)

            for j in range(heads):
                complete(j)

    @pl.when(jnp.logical_not(owner))
    def _():
        for j in range(heads):
            arrived(j)
            complete(j)

    for c in swap_x + swap_q:
        c.wait_send()

    @pl.when(jnp.logical_not(at_home))
    def _():
        for j in range(heads):
            for h in range(2):
                share(x, j, h).wait_send()

    for c in range(ncol):
        @pl.when(jnp.logical_and(owner, away(c)))
        def _():
            for j in range(heads):
                for h in range(2):
                    give(c, j, h).wait_send()

    @pl.when(up)
    def _():
        for j in range(heads):
            for h in range(2):
                chain(j, h).wait_send()


def solution(mesh):
    nrow, count = mesh.shape["row"], mesh.shape["frame"]
    ncol = columns_of(mesh)
    nz = count // ncol

    def body(latents, spatial_weights, causal_weights):
        _, band, cols, width = latents.shape
        maps, all_heads, size, _ = spatial_weights.shape
        heads = all_heads // nrow
        toks = nrow * band * cols
        bf, f32 = jnp.bfloat16, jnp.float32
        dma = pltpu.SemaphoreType.DMA
        peers = max(nrow - 1, 1)
        return pl.pallas_call(
            functools.partial(kernel, nrow, ncol, nz),
            out_shape=jax.ShapeDtypeStruct((1, band * nrow, cols, width // nrow), bf),
            in_specs=[pl.BlockSpec(memory_space=pltpu.HBM)] * 3,
            out_specs=pl.BlockSpec(memory_space=pltpu.VMEM),
            scratch_shapes=[
                pltpu.VMEM((nrow, band, cols, width), bf),
                pltpu.VMEM((maps, heads, size, size), bf),
                pltpu.VMEM((maps, heads, size, size), bf),
                pltpu.VMEM((heads, size, maps * LANES), bf),
                pltpu.VMEM((heads, toks, LANES), bf),
                pltpu.VMEM((toks, LANES), f32),
                pltpu.VMEM((nrow, toks, LANES), f32),
                pltpu.VMEM((heads, size, LANES), bf),
                pltpu.VMEM((ncol, heads, size, LANES), bf),
                pltpu.VMEM((heads, size, LANES), bf),
                pltpu.VMEM((heads, size, LANES), bf),
                pltpu.VMEM((heads, size, LANES), bf),
                pltpu.VMEM((ncol, heads, size, LANES), bf),
                pltpu.VMEM((heads, toks, LANES), bf),
                pltpu.VMEM((heads, toks, LANES), bf),
                pltpu.VMEM((heads, toks, LANES), bf),
                pltpu.VMEM((heads, toks, LANES), f32),
                pltpu.VMEM((heads, toks, LANES), f32),
                pltpu.VMEM((heads, LANES, LANES), f32),
                dma((3,)),
                dma((peers,)), dma((peers,)),
                dma((peers,)), dma((peers,)),
                dma((heads, 2)), dma((ncol, heads, 2)),
                dma((heads, 2)), dma((heads, 2)),
                dma((ncol, heads, 2)), dma((heads, 2)),
            ],
            compiler_params=pltpu.CompilerParams(
                collective_id=0, has_side_effects=True, vmem_limit_bytes=55_000_000),
        )(latents, spatial_weights, causal_weights)

    in_specs = (P(("group", "frame"), "row", None, None), P(), P())
    out_specs = P(("group", "frame"), None, None, "row")
    return jax.shard_map(body, mesh=mesh, in_specs=in_specs, out_specs=out_specs, check_vma=False)
```

```python
import functools

import jax
import jax.numpy as jnp
from jax import lax
from jax.experimental import pallas as pl
from jax.experimental.pallas import tpu as pltpu
from jax.sharding import PartitionSpec as P

MESH = pl.DeviceIdType.MESH
LANES = 128


def columns_of(mesh):
    count = mesh.shape["frame"]
    line = mesh.devices.reshape(mesh.shape["group"], count, mesh.shape["row"])[0, :, 0]
    places = [getattr(d, "coords", None) for d in line]
    if any(p is None or len(p) < 3 for p in places):
        return 2 if count % 2 == 0 else 1
    cols = 1
    while cols < count and places[cols][2] == places[0][2]:
        cols += 1
    return cols if count % cols == 0 else 1


def dot(a, b):
    return jnp.dot(a, b, preferred_element_type=jnp.float32)


def dot_t(a, b):
    return lax.dot_general(a, b, (((0,), (0,)), ((), ())), preferred_element_type=jnp.float32)


def kernel(nrow, ncol, nz, lat, sw, cw, out, xall, wsv, wcv, wj, xh, iv, sq, mine, sx, zin, zout, pin, pout, qs, ks, vs, vraw, gs, own,
           lsem, xsend, xrecv, qsend, qrecv, ssend, srecv, zsend, zrecv, psend, precv):
    heads, toks, _ = xh.shape
    size = wsv.shape[2]
    width = heads * nrow * size
    part = toks // nrow
    r = lax.axis_index("row")
    f = lax.axis_index("frame")
    z, x = lax.div(f, ncol), lax.rem(f, ncol)

    rows_peers = [lax.rem(r + d, nrow) for d in range(1, nrow)]

    spread = ncol >= nrow
    my_col, my_row = lax.rem(r, ncol), (nrow - 1 if spread else r)
    at_home = jnp.logical_and(x == my_col, r == my_row)
    held = x if spread else r
    owner = jnp.logical_and(r == nrow - 1, x < nrow) if spread else x == my_col
    up, down = jnp.logical_and(owner, z < nz - 1), jnp.logical_and(owner, z > 0)
    to_owner = {"frame": z * ncol + my_col, "row": my_row}

    def client(c):
        return {"frame": z * ncol + c, "row": lax.rem(held, nrow)}

    def away(c):
        return jnp.logical_not(jnp.logical_and(held == r, c == x))

    barrier = pltpu.get_barrier_semaphore()
    for p in rows_peers:
        pl.semaphore_signal(barrier, inc=1, device_id={"row": p}, device_id_type=MESH)

    @pl.when(jnp.logical_not(at_home))
    def _():
        pl.semaphore_signal(barrier, inc=1, device_id=to_owner, device_id_type=MESH)

    for c in range(ncol):
        @pl.when(jnp.logical_and(owner, away(c)))
        def _():
            pl.semaphore_signal(barrier, inc=1, device_id=client(c), device_id_type=MESH)

    @pl.when(down)
    def _():
        pl.semaphore_signal(barrier, inc=1, device_id={"frame": f - ncol}, device_id_type=MESH)

    @pl.when(up)
    def _():
        pl.semaphore_signal(barrier, inc=1, device_id={"frame": f + ncol}, device_id_type=MESH)

    get_x = pltpu.make_async_copy(lat.at[0], xall.at[r], lsem.at[0])
    get_s = pltpu.make_async_copy(sw.at[:, pl.ds(r * heads, heads)], wsv, lsem.at[1])
    get_c = pltpu.make_async_copy(cw.at[:, pl.ds(r * heads, heads)], wcv, lsem.at[2])
    get_x.start()
    get_s.start()
    get_c.start()

    @pl.when(z == 0)
    def _():
        zin[...] = jnp.zeros_like(zin)

    ends = jnp.where(z > 0, 1, 0) + jnp.where(z < nz - 1, 1, 0)
    clients = ncol - jnp.where(held == r, 1, 0)
    pl.semaphore_wait(barrier, (nrow - 1) + jnp.where(at_home, 0, 1) + jnp.where(owner, clients + ends, 0))

    swap_x = []
    for i, p in enumerate(rows_peers):
        c = pltpu.make_async_remote_copy(
            src_ref=lat.at[0], dst_ref=xall.at[r], send_sem=xsend.at[i], recv_sem=xrecv.at[i],
            device_id={"row": p}, device_id_type=MESH)
        c.start()
        swap_x.append(c)

    pad = jnp.zeros((part, LANES - size), jnp.bfloat16)
    wpad = jnp.zeros((size, LANES - size), jnp.bfloat16)

    def join(w, j):
        return jnp.concatenate([t for k in range(4) for t in (w[k, j], wpad)], axis=1)

    def project(u, w):
        m = dot(u[:, :size], w)
        q = jnp.maximum(m[:, :LANES], 0.0).astype(jnp.bfloat16)
        k = jnp.maximum(m[:, LANES:2 * LANES], 0.0).astype(jnp.bfloat16)
        return q, k, m[:, 2 * LANES:3 * LANES], m[:, 3 * LANES:]

    def stage(slot):
        rows = pl.ds(pl.multiple_of(slot * part, part), part)
        v = xall[slot].reshape(part, width)
        vf = v.astype(jnp.float32)
        inv = lax.rsqrt(jnp.sum(vf * vf, axis=-1, keepdims=True) * (1.0 / width) + 1e-06)
        inv = jnp.broadcast_to(inv, (part, LANES))
        iv[rows, :] = inv
        for rr in range(nrow):
            @pl.when(r == rr)
            def _():
                for j in range(heads):
                    lo = (rr * heads + j) * size
                    xh[j, rows, :] = jnp.concatenate([v[:, lo:lo + size], pad], axis=1)
        for j in range(heads):
            q, k, vv, g = project(xh[j, rows, :], wj[j])
            qs[j, rows, :] = q
            ks[j, rows, :] = k
            vs[j, rows, :] = (vv * (inv * inv)).astype(jnp.bfloat16)
            gs[j, rows, :] = jax.nn.sigmoid(g * inv)

    get_s.wait()
    for j in range(heads):
        wj[j] = join(wsv, j)
    get_x.wait()
    stage(r)
    for i, c in enumerate(swap_x):
        c.wait_recv()
        stage(lax.rem(r + (nrow - 1 - i), nrow))

    def attend(q, state):
        hi = state.astype(jnp.bfloat16)
        low = (state - hi.astype(jnp.float32)).astype(jnp.bfloat16)
        return dot(jnp.concatenate([q, q], axis=1), jnp.concatenate([hi, low], axis=0))

    def finish(base, g, a, inv):
        mean = jnp.sum(a * a, axis=-1, keepdims=True) * (1.0 / size)
        scale = inv * lax.rsqrt(mean * (inv * inv) + 1e-05)
        return (base.astype(jnp.float32) + g * a * scale).astype(jnp.bfloat16)

    total = jnp.zeros((toks, LANES), jnp.float32)
    for j in range(heads):
        mixed = finish(xh[j], gs[j], attend(qs[j], dot_t(ks[j], vs[j])), iv[...])
        xh[j] = mixed
        mf = mixed.astype(jnp.float32)
        total = total + mf * mf
    sq[r] = jnp.broadcast_to(jnp.sum(total, axis=-1, keepdims=True), (toks, LANES))

    swap_q = []
    for i, p in enumerate(rows_peers):
        c = pltpu.make_async_remote_copy(
            src_ref=sq.at[r], dst_ref=sq.at[r], send_sem=qsend.at[i], recv_sem=qrecv.at[i],
            device_id={"row": p}, device_id_type=MESH)
        c.start()
        swap_q.append(c)
    get_c.wait()
    for j in range(heads):
        q, k, vv, g = project(xh[j], join(wcv, j))
        qs[j] = q
        ks[j] = k
        vraw[j] = vv
        gs[j] = g
    for c in swap_q:
        c.wait_recv()
    inv_c = lax.rsqrt(jnp.sum(sq[...], axis=0) * (1.0 / width) + 1e-06)
    iv[...] = inv_c

    tiles, pieces = size // 16, zsend.shape[1]
    edges = [16 * ((tiles * i + pieces - 1) // pieces) for i in range(pieces)] + [size]
    chunks = [(a, b - a) for a, b in zip(edges[:-1], edges[1:])]

    def share(c, j, h):
        rows = pl.ds(*chunks[h])
        return pltpu.make_async_remote_copy(
            src_ref=mine.at[j, rows], dst_ref=sx.at[c, j, rows], send_sem=ssend.at[j, h],
            recv_sem=srecv.at[c, j, h], device_id=to_owner, device_id_type=MESH)

    def chain(j, h):
        rows = pl.ds(*chunks[h])
        return pltpu.make_async_remote_copy(
            src_ref=zout.at[j, rows], dst_ref=zin.at[j, rows], send_sem=zsend.at[j, h],
            recv_sem=zrecv.at[j, h], device_id={"frame": lax.rem(f + ncol, ncol * nz)}, device_id_type=MESH)

    def give(c, j, h):
        rows = pl.ds(*chunks[h])
        return pltpu.make_async_remote_copy(
            src_ref=pout.at[c, j, rows], dst_ref=pin.at[j, rows], send_sem=psend.at[c, j, h],
            recv_sem=precv.at[j, h], device_id=client(c), device_id_type=MESH)

    for j in range(heads):
        state = dot_t(ks[j], (vraw[j] * (inv_c * inv_c)).astype(jnp.bfloat16))
        mine[j] = state[:size].astype(jnp.bfloat16)

        @pl.when(at_home)
        def _():
            sx[x, j] = mine[j]

        @pl.when(jnp.logical_not(at_home))
        def _():
            for h in range(pieces):
                share(x, j, h).start()
        own[j] = state

    for j in range(heads):
        gs[j] = jax.nn.sigmoid(gs[j] * inv_c)
        vraw[j] = attend(qs[j], own[j])

    @pl.when(owner)
    def _():
        for j in range(heads):
            for h in range(pieces):
                rows = pl.ds(*chunks[h])
                for c in range(ncol):
                    @pl.when(away(c))
                    def _():
                        share(c, j, h).wait_recv()
                here = [sx[c, j, rows].astype(jnp.float32) for c in range(ncol)]

                @pl.when(down)
                def _():
                    chain(j, h).wait_recv()

                total = zin[j, rows].astype(jnp.float32)
                before = []
                for c in range(ncol):
                    before.append(total)
                    total = total + here[c]

                @pl.when(up)
                def _():
                    zout[j, rows] = total.astype(jnp.bfloat16)
                    chain(j, h).start()

                for c in range(ncol):
                    pout[c, j, rows] = before[c].astype(jnp.bfloat16)

                    @pl.when(away(c))
                    def _():
                        give(c, j, h).start()

    tail = jnp.zeros((LANES - size, LANES), jnp.bfloat16)
    def complete(j):
        a = vraw[j] + dot(qs[j], jnp.concatenate([pin[j], tail], axis=0))
        done = finish(xh[j], gs[j], a, iv[...])
        out[0, :, :, j * size:(j + 1) * size] = done[:, :size].reshape(out.shape[1:3] + (size,))

    @pl.when(owner)
    def _():
        @pl.when(at_home)
        def _():
            for j in range(heads):
                pin[j] = pout[x, j]

        @pl.when(jnp.logical_not(at_home))
        def _():
            for j in range(heads):
                for h in range(pieces):
                    give(x, j, h).wait_recv()

        for j in range(heads):
            complete(j)

    @pl.when(jnp.logical_not(owner))
    def _():
        for j in range(heads):
            for h in range(pieces):
                give(x, j, h).wait_recv()
            complete(j)

    for c in swap_x + swap_q:
        c.wait_send()

    @pl.when(jnp.logical_not(at_home))
    def _():
        for j in range(heads):
            for h in range(pieces):
                share(x, j, h).wait_send()

    for c in range(ncol):
        @pl.when(jnp.logical_and(owner, away(c)))
        def _():
            for j in range(heads):
                for h in range(pieces):
                    give(c, j, h).wait_send()

    @pl.when(up)
    def _():
        for j in range(heads):
            for h in range(pieces):
                chain(j, h).wait_send()


def solution(mesh):
    nrow, count = mesh.shape["row"], mesh.shape["frame"]
    ncol = columns_of(mesh)
    nz = count // ncol

    def body(latents, spatial_weights, causal_weights):
        _, band, cols, width = latents.shape
        maps, all_heads, size, _ = spatial_weights.shape
        heads = all_heads // nrow
        toks = nrow * band * cols
        bf, f32 = jnp.bfloat16, jnp.float32
        dma = pltpu.SemaphoreType.DMA
        peers, pieces = max(nrow - 1, 1), min(3, size // 16)
        return pl.pallas_call(
            functools.partial(kernel, nrow, ncol, nz),
            out_shape=jax.ShapeDtypeStruct((1, band * nrow, cols, width // nrow), bf),
            in_specs=[pl.BlockSpec(memory_space=pltpu.HBM)] * 3,
            out_specs=pl.BlockSpec(memory_space=pltpu.VMEM),
            scratch_shapes=[
                pltpu.VMEM((nrow, band, cols, width), bf),
                pltpu.VMEM((maps, heads, size, size), bf),
                pltpu.VMEM((maps, heads, size, size), bf),
                pltpu.VMEM((heads, size, maps * LANES), bf),
                pltpu.VMEM((heads, toks, LANES), bf),
                pltpu.VMEM((toks, LANES), f32),
                pltpu.VMEM((nrow, toks, LANES), f32),
                pltpu.VMEM((heads, size, LANES), bf),
                pltpu.VMEM((ncol, heads, size, LANES), bf),
                pltpu.VMEM((heads, size, LANES), bf),
                pltpu.VMEM((heads, size, LANES), bf),
                pltpu.VMEM((heads, size, LANES), bf),
                pltpu.VMEM((ncol, heads, size, LANES), bf),
                pltpu.VMEM((heads, toks, LANES), bf),
                pltpu.VMEM((heads, toks, LANES), bf),
                pltpu.VMEM((heads, toks, LANES), bf),
                pltpu.VMEM((heads, toks, LANES), f32),
                pltpu.VMEM((heads, toks, LANES), f32),
                pltpu.VMEM((heads, LANES, LANES), f32),
                dma((3,)),
                dma((peers,)), dma((peers,)),
                dma((peers,)), dma((peers,)),
                dma((heads, pieces)), dma((ncol, heads, pieces)),
                dma((heads, pieces)), dma((heads, pieces)),
                dma((ncol, heads, pieces)), dma((heads, pieces)),
            ],
            compiler_params=pltpu.CompilerParams(
                collective_id=0, has_side_effects=True, vmem_limit_bytes=60_000_000),
        )(latents, spatial_weights, causal_weights)

    in_specs = (P(("group", "frame"), "row", None, None), P(), P())
    out_specs = P(("group", "frame"), None, None, "row")
    return jax.shard_map(body, mesh=mesh, in_specs=in_specs, out_specs=out_specs, check_vma=False)
```

```python
import functools

import jax
import jax.numpy as jnp
from jax import lax
from jax.experimental import pallas as pl
from jax.experimental.pallas import tpu as pltpu
from jax.sharding import PartitionSpec as P

MESH = pl.DeviceIdType.MESH
LANES = 128


def columns_of(mesh):
    count = mesh.shape["frame"]
    line = mesh.devices.reshape(mesh.shape["group"], count, mesh.shape["row"])[0, :, 0]
    places = [getattr(d, "coords", None) for d in line]
    if any(p is None or len(p) < 3 for p in places):
        return 2 if count % 2 == 0 else 1
    cols = 1
    while cols < count and places[cols][2] == places[0][2]:
        cols += 1
    return cols if count % cols == 0 else 1


def dot(a, b):
    return jnp.dot(a, b, preferred_element_type=jnp.float32)


def dot_t(a, b):
    return lax.dot_general(a, b, (((0,), (0,)), ((), ())), preferred_element_type=jnp.float32)


def kernel(nrow, ncol, nz, lat, sw, cw, out, xall, wsv, wcv, wj, xh, iv, sq, mine, sx, zin, zout, pin, pout, qs, ks, vs, vraw, gs, own,
           lsem, xsend, xrecv, qsend, qrecv, ssend, srecv, zsend, zrecv, psend, precv):
    heads, toks, _ = xh.shape
    size = wsv.shape[2]
    width = heads * nrow * size
    part = toks // nrow
    r = lax.axis_index("row")
    f = lax.axis_index("frame")
    z, x = lax.div(f, ncol), lax.rem(f, ncol)

    rows_peers = [lax.rem(r + d, nrow) for d in range(1, nrow)]

    spread = ncol >= nrow
    my_col, my_row = lax.rem(r, ncol), (nrow - 1 if spread else r)
    at_home = jnp.logical_and(x == my_col, r == my_row)
    held = x if spread else r
    owner = jnp.logical_and(r == nrow - 1, x < nrow) if spread else x == my_col
    up, down = jnp.logical_and(owner, z < nz - 1), jnp.logical_and(owner, z > 0)
    to_owner = {"frame": z * ncol + my_col, "row": my_row}

    def client(c):
        return {"frame": z * ncol + c, "row": lax.rem(held, nrow)}

    def away(c):
        return jnp.logical_not(jnp.logical_and(held == r, c == x))

    barrier = pltpu.get_barrier_semaphore()
    for p in rows_peers:
        pl.semaphore_signal(barrier, inc=1, device_id={"row": p}, device_id_type=MESH)

    @pl.when(jnp.logical_not(at_home))
    def _():
        pl.semaphore_signal(barrier, inc=1, device_id=to_owner, device_id_type=MESH)

    for c in range(ncol):
        @pl.when(jnp.logical_and(owner, away(c)))
        def _():
            pl.semaphore_signal(barrier, inc=1, device_id=client(c), device_id_type=MESH)

    @pl.when(down)
    def _():
        pl.semaphore_signal(barrier, inc=1, device_id={"frame": f - ncol}, device_id_type=MESH)

    @pl.when(up)
    def _():
        pl.semaphore_signal(barrier, inc=1, device_id={"frame": f + ncol}, device_id_type=MESH)

    get_x = pltpu.make_async_copy(lat.at[0], xall.at[r], lsem.at[0])
    get_s = pltpu.make_async_copy(sw.at[:, pl.ds(r * heads, heads)], wsv, lsem.at[1])
    get_c = pltpu.make_async_copy(cw.at[:, pl.ds(r * heads, heads)], wcv, lsem.at[2])
    get_x.start()
    get_s.start()
    get_c.start()

    @pl.when(z == 0)
    def _():
        zin[...] = jnp.zeros_like(zin)

    ends = jnp.where(z > 0, 1, 0) + jnp.where(z < nz - 1, 1, 0)
    clients = ncol - jnp.where(held == r, 1, 0)
    pl.semaphore_wait(barrier, (nrow - 1) + jnp.where(at_home, 0, 1) + jnp.where(owner, clients + ends, 0))

    swap_x = []
    for i, p in enumerate(rows_peers):
        c = pltpu.make_async_remote_copy(
            src_ref=lat.at[0], dst_ref=xall.at[r], send_sem=xsend.at[i], recv_sem=xrecv.at[i],
            device_id={"row": p}, device_id_type=MESH)
        c.start()
        swap_x.append(c)

    pad = jnp.zeros((part, LANES - size), jnp.bfloat16)
    wpad = jnp.zeros((size, LANES - size), jnp.bfloat16)

    def join(w, j):
        return jnp.concatenate([t for k in range(4) for t in (w[k, j], wpad)], axis=1)

    def project(u, w):
        m = dot(u[:, :size], w)
        q = jnp.maximum(m[:, :LANES], 0.0).astype(jnp.bfloat16)
        k = jnp.maximum(m[:, LANES:2 * LANES], 0.0).astype(jnp.bfloat16)
        return q, k, m[:, 2 * LANES:3 * LANES], m[:, 3 * LANES:]

    def stage(slot):
        rows = pl.ds(pl.multiple_of(slot * part, part), part)
        v = xall[slot].reshape(part, width)
        vf = v.astype(jnp.float32)
        inv = lax.rsqrt(jnp.sum(vf * vf, axis=-1, keepdims=True) * (1.0 / width) + 1e-06)
        inv = jnp.broadcast_to(inv, (part, LANES))
        iv[rows, :] = inv
        for rr in range(nrow):
            @pl.when(r == rr)
            def _():
                for j in range(heads):
                    lo = (rr * heads + j) * size
                    xh[j, rows, :] = jnp.concatenate([v[:, lo:lo + size], pad], axis=1)
        for j in range(heads):
            q, k, vv, g = project(xh[j, rows, :], wj[j])
            qs[j, rows, :] = q
            ks[j, rows, :] = k
            vs[j, rows, :] = (vv * (inv * inv)).astype(jnp.bfloat16)
            gs[j, rows, :] = jax.nn.sigmoid(g * inv)

    get_s.wait()
    for j in range(heads):
        wj[j] = join(wsv, j)
    get_x.wait()
    stage(r)
    for i, c in enumerate(swap_x):
        c.wait_recv()
        stage(lax.rem(r + (nrow - 1 - i), nrow))

    def attend(q, state):
        hi = state.astype(jnp.bfloat16)
        low = (state - hi.astype(jnp.float32)).astype(jnp.bfloat16)
        return dot(jnp.concatenate([q, q], axis=1), jnp.concatenate([hi, low], axis=0))

    def finish(base, g, a, inv):
        mean = jnp.sum(a * a, axis=-1, keepdims=True) * (1.0 / size)
        scale = inv * lax.rsqrt(mean * (inv * inv) + 1e-05)
        return (base.astype(jnp.float32) + g * a * scale).astype(jnp.bfloat16)

    total = jnp.zeros((toks, LANES), jnp.float32)
    for j in range(heads):
        mixed = finish(xh[j], gs[j], attend(qs[j], dot_t(ks[j], vs[j])), iv[...])
        xh[j] = mixed
        mf = mixed.astype(jnp.float32)
        total = total + mf * mf
    sq[r] = jnp.broadcast_to(jnp.sum(total, axis=-1, keepdims=True), (toks, LANES))

    swap_q = []
    for i, p in enumerate(rows_peers):
        c = pltpu.make_async_remote_copy(
            src_ref=sq.at[r], dst_ref=sq.at[r], send_sem=qsend.at[i], recv_sem=qrecv.at[i],
            device_id={"row": p}, device_id_type=MESH)
        c.start()
        swap_q.append(c)
    get_c.wait()
    for j in range(heads):
        q, k, vv, g = project(xh[j], join(wcv, j))
        qs[j] = q
        ks[j] = k
        vraw[j] = vv
        gs[j] = g
    for c in swap_q:
        c.wait_recv()
    inv_c = lax.rsqrt(jnp.sum(sq[...], axis=0) * (1.0 / width) + 1e-06)
    iv[...] = inv_c

    cut = (size // 2 + 15) // 16 * 16
    chunks = [(0, cut), (cut, size - cut)]

    def share(c, j, h):
        rows = pl.ds(*chunks[h])
        return pltpu.make_async_remote_copy(
            src_ref=mine.at[j, rows], dst_ref=sx.at[c, j, rows], send_sem=ssend.at[j, h],
            recv_sem=srecv.at[c, j, h], device_id=to_owner, device_id_type=MESH)

    def chain(j, h):
        rows = pl.ds(*chunks[h])
        return pltpu.make_async_remote_copy(
            src_ref=zout.at[j, rows], dst_ref=zin.at[j, rows], send_sem=zsend.at[j, h],
            recv_sem=zrecv.at[j, h], device_id={"frame": lax.rem(f + ncol, ncol * nz)}, device_id_type=MESH)

    def give(c, j, h):
        rows = pl.ds(*chunks[h])
        return pltpu.make_async_remote_copy(
            src_ref=pout.at[c, j, rows], dst_ref=pin.at[j, rows], send_sem=psend.at[c, j, h],
            recv_sem=precv.at[j, h], device_id=client(c), device_id_type=MESH)

    for j in range(heads):
        state = dot_t(ks[j], (vraw[j] * (inv_c * inv_c)).astype(jnp.bfloat16))
        mine[j] = state[:size].astype(jnp.bfloat16)

        @pl.when(at_home)
        def _():
            sx[x, j] = mine[j]

        @pl.when(jnp.logical_not(at_home))
        def _():
            for h in range(2):
                share(x, j, h).start()
        own[j] = state

    def collect(j, h):
        for c in range(ncol):
            @pl.when(away(c))
            def _():
                share(c, j, h).wait_recv()

        @pl.when(down)
        def _():
            chain(j, h).wait_recv()

    @pl.when(up)
    def _():
        for j in range(heads):
            for h in range(2):
                rows = pl.ds(*chunks[h])
                collect(j, h)
                total = zin[j, rows].astype(jnp.float32)
                for c in range(ncol):
                    total = total + sx[c, j, rows].astype(jnp.float32)
                zout[j, rows] = total.astype(jnp.bfloat16)
                chain(j, h).start()

    @pl.when(owner)
    def _():
        for j in range(heads):
            for h in range(2):
                rows = pl.ds(*chunks[h])

                @pl.when(z == nz - 1)
                def _():
                    collect(j, h)

                before = zin[j, rows].astype(jnp.float32)
                for c in range(ncol):
                    pout[c, j, rows] = before.astype(jnp.bfloat16)

                    @pl.when(away(c))
                    def _():
                        give(c, j, h).start()
                    before = before + sx[c, j, rows].astype(jnp.float32)

    for j in range(heads):
        gs[j] = jax.nn.sigmoid(gs[j] * inv_c)
        vraw[j] = attend(qs[j], own[j])

    tail = jnp.zeros((LANES - size, LANES), jnp.bfloat16)
    for j in range(heads):
        @pl.when(at_home)
        def _():
            pin[j] = pout[x, j]

        @pl.when(jnp.logical_not(at_home))
        def _():
            for h in range(2):
                give(x, j, h).wait_recv()

        a = vraw[j] + dot(qs[j], jnp.concatenate([pin[j], tail], axis=0))
        done = finish(xh[j], gs[j], a, iv[...])
        out[0, :, :, j * size:(j + 1) * size] = done[:, :size].reshape(out.shape[1:3] + (size,))

    for c in swap_x + swap_q:
        c.wait_send()

    @pl.when(jnp.logical_not(at_home))
    def _():
        for j in range(heads):
            for h in range(2):
                share(x, j, h).wait_send()

    for c in range(ncol):
        @pl.when(jnp.logical_and(owner, away(c)))
        def _():
            for j in range(heads):
                for h in range(2):
                    give(c, j, h).wait_send()

    @pl.when(up)
    def _():
        for j in range(heads):
            for h in range(2):
                chain(j, h).wait_send()


def solution(mesh):
    nrow, count = mesh.shape["row"], mesh.shape["frame"]
    ncol = columns_of(mesh)
    nz = count // ncol

    def body(latents, spatial_weights, causal_weights):
        _, band, cols, width = latents.shape
        maps, all_heads, size, _ = spatial_weights.shape
        heads = all_heads // nrow
        toks = nrow * band * cols
        bf, f32 = jnp.bfloat16, jnp.float32
        dma = pltpu.SemaphoreType.DMA
        peers = max(nrow - 1, 1)
        return pl.pallas_call(
            functools.partial(kernel, nrow, ncol, nz),
            out_shape=jax.ShapeDtypeStruct((1, band * nrow, cols, width // nrow), bf),
            in_specs=[pl.BlockSpec(memory_space=pltpu.HBM)] * 3,
            out_specs=pl.BlockSpec(memory_space=pltpu.VMEM),
            scratch_shapes=[
                pltpu.VMEM((nrow, band, cols, width), bf),
                pltpu.VMEM((maps, heads, size, size), bf),
                pltpu.VMEM((maps, heads, size, size), bf),
                pltpu.VMEM((heads, size, maps * LANES), bf),
                pltpu.VMEM((heads, toks, LANES), bf),
                pltpu.VMEM((toks, LANES), f32),
                pltpu.VMEM((nrow, toks, LANES), f32),
                pltpu.VMEM((heads, size, LANES), bf),
                pltpu.VMEM((ncol, heads, size, LANES), bf),
                pltpu.VMEM((heads, size, LANES), bf),
                pltpu.VMEM((heads, size, LANES), bf),
                pltpu.VMEM((heads, size, LANES), bf),
                pltpu.VMEM((ncol, heads, size, LANES), bf),
                pltpu.VMEM((heads, toks, LANES), bf),
                pltpu.VMEM((heads, toks, LANES), bf),
                pltpu.VMEM((heads, toks, LANES), bf),
                pltpu.VMEM((heads, toks, LANES), f32),
                pltpu.VMEM((heads, toks, LANES), f32),
                pltpu.VMEM((heads, LANES, LANES), f32),
                dma((3,)),
                dma((peers,)), dma((peers,)),
                dma((peers,)), dma((peers,)),
                dma((heads, 2)), dma((ncol, heads, 2)),
                dma((heads, 2)), dma((heads, 2)),
                dma((ncol, heads, 2)), dma((heads, 2)),
            ],
            compiler_params=pltpu.CompilerParams(
                collective_id=0, has_side_effects=True, vmem_limit_bytes=55_000_000),
        )(latents, spatial_weights, causal_weights)

    in_specs = (P(("group", "frame"), "row", None, None), P(), P())
    out_specs = P(("group", "frame"), None, None, "row")
    return jax.shard_map(body, mesh=mesh, in_specs=in_specs, out_specs=out_specs, check_vma=False)
```
